32 devices in a mesh: groups: 2 (over y), ctx: 4 (over z), chan: 4 (over x, core).
Axes of the slice: x: 2, y: 2, z: 4, core: 2. Of those that a mesh axis runs over, the one named last changes fastest.
Arguments:
- q_feat: bfloat16 [4096, 8192], P(('groups', 'ctx'), 'chan'), parts along dimension 0, may hold values from -6 to 6
- k_feat: bfloat16 [4096, 8192], P(('groups', 'ctx'), 'chan'), parts along dimension 0, may hold values from -6 to 6
- v_feat: bfloat16 [4096, 8192], P(('groups', 'ctx'), 'chan'), parts along dimension 0, may hold values from -6 to 6
- pole_rate: float32 [16, 8192], P(None, 'chan'), may hold values from 4.8828126e-05 to 0.03
- residue: float32 [16, 8192], P(None, 'chan'), may hold values from -1.5 to 1.5
- skip_gain: float32 [8192], P('chan'), may hold values from 0.5 to 1.5
- lengths: int32 [8], P('groups'), parts along dimension 0, may hold values from 1 to 1024, 2048 in all
- owners: int32 [8], P('groups'), parts along dimension 0, may hold values from 0 to 3, as said below
Outputs:
- mixed_out: bfloat16 [4096, 8192], P(('groups', 'ctx'), 'chan'), parts along dimension 0
- decode_state: float32 [8, 16, 8192], P(('groups', 'ctx'), None, 'chan'), parts along dimension 0
The draws below stay inside these ranges and needn't reach their ends.
There are 2 independent parts, one for each index of `groups`. The reference program is written for one: setup_inputs(seed, part) draws one part's arguments, and reference() takes and returns one part's arrays. A program takes and returns all parts, laid end to end along the dimension named above; an argument that names none is the same for every part. Nothing has to cross between parts.
Inputs may be any that keep to these rules, and one draw needn't show every extreme that they name: The 4 lengths sum to 2048; the longest is exactly 1024. The 4 owners are distinct.
All inputs are finite; a program needn't handle non-finite values.
Results may differ from the reference program's by a relative error of at most 0.001.
Values sent between devices are 32-bit elements; how exact they have to be, the bound alone decides.
No kernel may reach another device: no remote copies, remote signals or barrier semaphores. Data moves between devices by JAX's collectives and lax.ppermute only.
A program may use at most 128 MiB of HBM per device.

```python
import math
import jax
import jax.numpy as jnp
import numpy as np
from jax import lax

D = 8192
POLES = 16
REQS = 4
TOKENS = 2048
OWNER_SLOTS = 4
N_CTX = 4


def draw_owners(key, part):
    middle = 1 + jax.random.permutation(jax.random.fold_in(key, 17), N_CTX - 2)[:REQS - 2]
    values = jnp.concatenate([jnp.array([N_CTX - 1, 0], jnp.int32), middle.astype(jnp.int32)])
    order = jax.random.permutation(jax.random.fold_in(key, 23), REQS)
    return values[order].astype(jnp.int32)


def block_levels(rng, dims, shards, smallest, top_value):
    factor_of, own = 1.0, jax.random.fold_in(rng, 6)
    for dim, parts in shards:
        draws = jnp.exp(jax.random.uniform(jax.random.fold_in(own, dim), (parts,), jnp.float32, smallest / len(shards), top_value / len(shards)))
        factor_of = factor_of * jnp.repeat(draws, dims[dim] // parts).reshape([-1 if axis == dim else 1 for axis in range(len(dims))])
    return factor_of


def length_profile(amount, total, most, slope):
    loads = [(1 << 20) // math.isqrt(standing ** slope) + 1 for standing in range(2, amount + 1)]
    spare, holding = total - most - (amount - 1), [1] * (amount - 1)
    while spare > 0:
        free = [i for i in range(amount - 1) if holding[i] < most]
        whole, remaining = sum([loads[i] for i in free]), spare
        for i in free:
            more = min(most - holding[i], max(1, remaining * loads[i] // whole), spare)
            holding[i] = holding[i] + more
            spare = spare - more
    return np.array([most] + holding)


def ragged_sizes(stream_key, number_of, total, most, lean):
    if number_of == 2:
        one = jax.random.randint(stream_key, (), max(1, total - most), min(most, total - 1) + 1)
        return jnp.stack([one, total - one])
    sizes = jnp.asarray(length_profile(number_of, total, most, lean), jnp.int32)
    twos = (number_of - 1) // 2
    giver, receiver = sizes[1:1 + 2 * twos:2], sizes[2:2 + 2 * twos:2]
    margin = jnp.minimum(giver - 1, most - receiver)
    moved = jax.random.randint(jax.random.fold_in(stream_key, 1), (twos,), 0, 1 << 20) % (margin + 1)
    sizes = sizes.at[1:1 + 2 * twos:2].set(giver - moved).at[2:2 + 2 * twos:2].set(receiver + moved)
    return sizes[jax.random.permutation(jax.random.fold_in(stream_key, 2), number_of)]


def centred(rng, extent, width, most, pieces=(), held_as=jnp.bfloat16):
    values = width * jax.random.normal(rng, extent, jnp.float32)
    if pieces:
        values = values * block_levels(rng, extent, pieces, -0.22, 0.18)
    return jnp.clip(values, -most, most).astype(held_as)


def setup_inputs(seed: int = 0, part: int = 0) -> dict:
    splits = jax.random.split(jax.random.key(seed), 9)
    part_splits = jax.random.split(jax.random.fold_in(splits[8], part), 9)
    q_feat = centred(part_splits[0], (TOKENS, D), 1.0, 6.0, ((0, 4), (1, 4)))
    k_feat = centred(part_splits[1], (TOKENS, D), 1.0, 6.0, ((0, 4), (1, 4)))
    v_feat = centred(part_splits[2], (TOKENS, D), 1.0, 6.0, ((0, 4), (1, 4)))
    pole_rate = jnp.clip(jnp.exp(math.log(0.03) - 6.420646 * jax.random.uniform(splits[3], (POLES, D), jnp.float32) ** block_levels(splits[3], (POLES, D), ((1, 4),), -0.2, 0.2)), 4.882812572759576e-05, 0.03)
    residue = centred(splits[4], (POLES, D), 0.25, 1.5, ((1, 4),), jnp.float32)
    skip_gain = jnp.clip(0.5 + 1.0 * jax.random.uniform(splits[5], (D,), jnp.float32) ** block_levels(splits[5], (D,), ((0, 4),), -0.2, 0.2), 0.5, 1.5)
    lengths = ragged_sizes(part_splits[6], REQS, TOKENS, TOKENS // 2, 2).astype(jnp.int32)
    owners = draw_owners(jax.random.fold_in(jax.random.fold_in(splits[8], part), 71), part)
    return dict(q_feat=q_feat, k_feat=k_feat, v_feat=v_feat, pole_rate=pole_rate, residue=residue, skip_gain=skip_gain, lengths=lengths, owners=owners)


def reference(q_feat, k_feat, v_feat, pole_rate, residue, skip_gain, lengths, owners):
    mixed_in = k_feat.astype(jnp.float32) * v_feat.astype(jnp.float32)
    offsets = (jnp.cumsum(lengths) - lengths).astype(jnp.int32)
    positions = jnp.arange(TOKENS, dtype=jnp.int32)
    segment = (lax.optimization_barrier(jnp.sum((positions[:, None] >= offsets[None, :]).astype(jnp.int32), axis=1)) - 1).astype(jnp.int32)
    is_start = positions == offsets[segment]
    pole_decay = jnp.exp(-pole_rate)
    scaled_res = residue * jnp.sqrt(1.0 - jnp.exp(-2.0 * pole_rate))

    def advance(loop_carry, inputs_now):
        mode_state, store = loop_carry
        row_in, seg_now, start_now = inputs_now
        mode_state = jnp.where(start_now, jnp.zeros_like(mode_state), pole_decay * mode_state) + row_in[None, :]
        store = store.at[seg_now].set(mode_state)
        return ((mode_state, store), lax.optimization_barrier(jnp.sum(scaled_res * mode_state, axis=0)))
    init_state = jnp.zeros((POLES, D), jnp.float32)
    init_store = jnp.zeros((REQS, POLES, D), jnp.float32)
    (last_state, store), conv = lax.scan(advance, (init_state, init_store), (mixed_in, segment, is_start))
    mixed_out = (q_feat.astype(jnp.float32) * (conv + skip_gain[None, :] * mixed_in)).astype(jnp.bfloat16)
    decode_state = jnp.zeros((OWNER_SLOTS, POLES, D), jnp.float32).at[owners.astype(jnp.int32)].set(store)
    return (mixed_out, decode_state)
```

```python
import functools

import jax
import jax.numpy as jnp
from jax import lax
from jax.experimental import pallas as pl
from jax.experimental.pallas import tpu as pltpu
from jax.sharding import PartitionSpec as P

LANES = 128
SUBS = 8
CHUNK = 64
UNROLL = 8
VMEM_BYTES = 40 * 1024 * 1024


def request_span(lengths_ref, request, request_count):
    start = jnp.int32(0)
    length = jnp.int32(0)
    for r in range(request_count):
        start = start + jnp.where(r < request, lengths_ref[r], 0)
        length = length + jnp.where(r == request, lengths_ref[r], 0)
    return start, start + length - 1


def request_at(lengths_ref, position, request_count):
    index = jnp.int32(-1)
    start = jnp.int32(0)
    for r in range(request_count):
        index = index + (start <= position).astype(jnp.int32)
        start = start + lengths_ref[r]
    return index


def token_loop(lo, hi, step, carry):
    count = jnp.maximum(hi - lo, 0)
    groups = lax.div(count, jnp.int32(UNROLL))

    def many(g, carry):
        base = lo + g * UNROLL
        for s in range(UNROLL):
            carry = step(base + s, carry)
        return carry

    carry = lax.fori_loop(0, groups, many, carry)
    return lax.fori_loop(lo + groups * UNROLL, lo + count, step, carry)


def to_rows(value_ref, rows_ref, tiles, change=lambda x: x):
    pole_count = value_ref.shape[0]
    span = max(tiles, SUBS)
    for pt in range(pole_count // SUBS):
        for j in range(tiles):
            tile = value_ref[pt * SUBS : (pt + 1) * SUBS, j * LANES : (j + 1) * LANES]
            rows_ref[pl.ds(pt * SUBS * span + j, SUBS, stride=span), :] = change(tile)


def chunk_copies(pairs, sems, c):
    rows = pl.ds(pl.multiple_of(c * CHUNK, CHUNK), CHUNK)
    return [
        pltpu.make_async_copy(src.at[rows, :], dst.at[rows, :], sems.at[n, c])
        for n, (src, dst) in enumerate(pairs)
    ]


def fill_rows(k_buf, v_buf, u_rows, c, tiles):
    span = max(tiles, SUBS)

    def block(b, _):
        rows = pl.ds(pl.multiple_of(c * CHUNK + b * 16, 16), 16)
        for j in range(tiles):
            lanes = slice(j * LANES, (j + 1) * LANES)
            u = k_buf[rows, lanes].astype(jnp.float32) * v_buf[rows, lanes].astype(jnp.float32)
            for half in range(2):
                u_rows[pl.ds((b * 16 + half * SUBS) * span + j, SUBS, stride=span), :] = u[
                    half * SUBS : (half + 1) * SUBS
                ]
        return 0

    lax.fori_loop(0, CHUNK // 16, block, 0)


def row_at(row, h, span):
    return pl.ds(pl.multiple_of(row * span + h * SUBS, SUBS), SUBS)


def row_tile(ref, row, h, span):
    return ref[row_at(row, h, span), :]


def pieces_kernel(
    request_count, lengths_ref, owners_ref, k_hbm, v_hbm, rate_ref, *rest
):
    n = lax.axis_size("ctx")
    i = lax.axis_index("ctx")
    far_count = n - 3
    even_ref, odd_ref, next_ref, own_ref = rest[:4]
    far_refs = rest[4 : 4 + far_count]
    k_buf, v_buf, u_rows, a_rows, states, sems = rest[4 + far_count :]
    pole_count, channels = rate_ref.shape
    tok_dev = k_buf.shape[0]
    tiles = channels // LANES
    span = max(tiles, SUBS)
    halves = span // SUBS
    chunks = tok_dev // CHUNK
    first = i * tok_dev
    last = first + tok_dev - 1
    moves = ((k_hbm, k_buf), (v_hbm, v_buf))
    for c in range(chunks):
        for copy in chunk_copies(moves, sems, c):
            copy.start()
    to_rows(rate_ref, a_rows, tiles, lambda x: jnp.exp(-x))

    def clear(b, _):
        states[pl.ds(pl.multiple_of(b * SUBS, SUBS), SUBS), :] = jnp.zeros((SUBS, LANES), jnp.float32)
        return 0

    lax.fori_loop(0, request_count * pole_count * halves, clear, 0)

    def chunk(c, _):
        for copy in chunk_copies(moves, sems, c):
            copy.wait()
        fill_rows(k_buf, v_buf, u_rows, c, tiles)
        base = first + c * CHUNK

        def request(r, start):
            length = lengths_ref[r]
            lo = jnp.maximum(start - base, 0)
            hi = jnp.minimum(start + length - base, CHUNK)

            @pl.when(hi > lo)
            def _():
                def half(h, _):
                    decay = [row_tile(a_rows, p, h, span) for p in range(pole_count)]
                    state = tuple(
                        row_tile(states, r * pole_count + p, h, span) for p in range(pole_count)
                    )

                    def step(t, state):
                        u = row_tile(u_rows, t, h, span)
                        return tuple(s * a + u for s, a in zip(state, decay))

                    state = token_loop(lo, hi, step, state)
                    for p in range(pole_count):
                        states[row_at(r * pole_count + p, h, span), :] = state[p]
                    return 0

                lax.fori_loop(0, halves, half, 0)

            return start + length

        lax.fori_loop(0, request_count, request, jnp.int32(0))
        return 0

    lax.fori_loop(0, chunks, chunk, 0)

    def owned(slot):
        request = jnp.int32(0)
        found = jnp.int32(0)
        for r in range(request_count):
            match = (owners_ref[r] == slot).astype(jnp.int32)
            request = request + r * match
            found = found + match
        start, end = request_span(lengths_ref, request, request_count)
        live = (found > 0) & (start <= last) & (end >= first)
        return request, jnp.maximum(end - last, 0), live

    def emit(out_ref, what):
        request, steps, live = what
        rate_scale = -steps.astype(jnp.float32)
        keep = jnp.where(live, 1.0, 0.0).astype(jnp.float32)
        for pt in range(pole_count // SUBS):
            for j in range(tiles):
                rows = slice(pt * SUBS, (pt + 1) * SUBS)
                lanes = slice(j * LANES, (j + 1) * LANES)
                state = states[
                    pl.ds((request * pole_count + pt * SUBS) * span + j, SUBS, stride=span), :
                ]
                out_ref[rows, lanes] = state * (jnp.exp(rate_ref[rows, lanes] * rate_scale) * keep)

    def pick(flag, yes, no):
        return tuple(jnp.where(flag, a, b) for a, b in zip(yes, no))

    odd = lax.rem(i, 2) == 1
    crossing = (request_at(lengths_ref, last, request_count), jnp.int32(0), jnp.bool_(True))
    behind = owned(lax.rem(i + n - 1, n))
    ahead = owned(lax.rem(i + 1, n))
    emit(even_ref, pick(odd, behind, crossing))
    odd_forward = pick(i == n - 1, ahead, crossing)
    emit(odd_ref, pick(odd, odd_forward, behind))
    for d, far_ref in enumerate(far_refs):
        emit(far_ref, owned(lax.rem(i + 2 + d, n)))
    emit(next_ref, ahead)
    emit(own_ref, owned(i))


def local_kernel(
    request_count,
    lengths_ref,
    k_hbm,
    v_hbm,
    rate_ref,
    residue_ref,
    skip_ref,
    out_hbm,
    k_buf,
    v_buf,
    out_buf,
    u_rows,
    y_rows,
    a_rows,
    r_rows,
    states,
    sems,
    out_sems,
):
    i = lax.axis_index("ctx")
    pole_count, channels = rate_ref.shape
    tok_dev = k_buf.shape[0]
    tiles = channels // LANES
    span = max(tiles, SUBS)
    halves = span // SUBS
    chunks = tok_dev // CHUNK
    first = i * tok_dev
    moves = ((k_hbm, k_buf), (v_hbm, v_buf))
    for c in range(chunks):
        for copy in chunk_copies(moves, sems, c):
            copy.start()
    to_rows(rate_ref, a_rows, tiles, lambda x: jnp.exp(-x))
    scaled_rows(rate_ref, residue_ref, r_rows, tiles)

    def chunk(c, _):
        for copy in chunk_copies(moves, sems, c):
            copy.wait()
        fill_rows(k_buf, v_buf, u_rows, c, tiles)
        base = first + c * CHUNK

        def request(r, start):
            length = lengths_ref[r]
            lo = jnp.maximum(start - base, 0)
            hi = jnp.minimum(start + length - base, CHUNK)

            @pl.when(hi > lo)
            def _():
                fresh = (start >= base) | (c == 0)

                def half(h, _):
                    decay = [row_tile(a_rows, p, h, span) for p in range(pole_count)]
                    gain = [row_tile(r_rows, p, h, span) for p in range(pole_count)]
                    state = tuple(
                        jnp.where(fresh, 0.0, row_tile(states, p, h, span))
                        for p in range(pole_count)
                    )

                    def step(t, state):
                        u = row_tile(u_rows, t, h, span)
                        state = tuple(s * a + u for s, a in zip(state, decay))
                        terms = [s * g for s, g in zip(state, gain)]
                        while len(terms) > 1:
                            terms = [x + y for x, y in zip(terms[::2], terms[1::2])]
                        y_rows[row_at(t, h, span), :] = terms[0]
                        return state

                    state = token_loop(lo, hi, step, state)
                    for p in range(pole_count):
                        states[row_at(p, h, span), :] = state[p]
                    return 0

                lax.fori_loop(0, halves, half, 0)

            return start + length

        lax.fori_loop(0, request_count, request, jnp.int32(0))

        def block(b, _):
            rows = pl.ds(pl.multiple_of(c * CHUNK + b * SUBS, SUBS), SUBS)
            for j in range(tiles):
                lanes = slice(j * LANES, (j + 1) * LANES)
                index = pl.ds(b * SUBS * span + j, SUBS, stride=span)
                out_buf[rows, lanes] = y_rows[index, :] + skip_ref[:, lanes] * u_rows[index, :]
            return 0

        lax.fori_loop(0, CHUNK // SUBS, block, 0)
        for copy in chunk_copies(((out_buf, out_hbm),), out_sems, c):
            copy.start()
        return 0

    lax.fori_loop(0, chunks, chunk, 0)
    for c in range(chunks):
        for copy in chunk_copies(((out_buf, out_hbm),), out_sems, c):
            copy.wait()


def scaled_rows(rate_ref, residue_ref, r_rows, tiles):
    pole_count = rate_ref.shape[0]
    span = max(tiles, SUBS)
    for pt in range(pole_count // SUBS):
        for j in range(tiles):
            rows = slice(pt * SUBS, (pt + 1) * SUBS)
            lanes = slice(j * LANES, (j + 1) * LANES)
            scaled = residue_ref[rows, lanes] * jnp.sqrt(
                1.0 - jnp.exp(-2.0 * rate_ref[rows, lanes])
            )
            r_rows[pl.ds(pt * SUBS * span + j, SUBS, stride=span), :] = scaled


def finish_kernel(
    request_count,
    hop_count,
    lengths_ref,
    w_hbm,
    q_hbm,
    rate_ref,
    residue_ref,
    *rest,
):
    hop_refs = rest[:hop_count]
    out_hbm, w_buf, q_buf, out_buf, y_rows, a_rows, z_rows, sems, out_sems = rest[hop_count:]
    i = lax.axis_index("ctx")
    pole_count, channels = rate_ref.shape
    tok_dev = w_buf.shape[0]
    tiles = channels // LANES
    span = max(tiles, SUBS)
    halves = span // SUBS
    chunks = tok_dev // CHUNK
    first = i * tok_dev
    moves = ((w_hbm, w_buf), (q_hbm, q_buf))
    for c in range(chunks):
        for copy in chunk_copies(moves, sems, c):
            copy.start()
    before = request_at(lengths_ref, first - 1, request_count)
    behind = request_at(lengths_ref, first - tok_dev - 1, request_count)
    _, end = request_span(lengths_ref, before, request_count)
    live = jnp.where(before < 0, 0, jnp.clip(end + 1 - first, 0, tok_dev))
    passed = (before >= 0) & (before == behind)
    to_rows(rate_ref, a_rows, tiles, lambda x: jnp.exp(-x))
    for pt in range(pole_count // SUBS):
        for j in range(tiles):
            rows = slice(pt * SUBS, (pt + 1) * SUBS)
            lanes = slice(j * LANES, (j + 1) * LANES)
            rate = rate_ref[rows, lanes]
            scaled = residue_ref[rows, lanes] * jnp.sqrt(1.0 - jnp.exp(-2.0 * rate))
            incoming = hop_refs[0][rows, lanes]
            for ref in hop_refs[1:]:
                incoming = incoming + jnp.where(passed, ref[rows, lanes], 0.0)
            z_rows[pl.ds(pt * SUBS * span + j, SUBS, stride=span), :] = (
                incoming * scaled * jnp.exp(-rate)
            )

    def chunk(c, _):
        for copy in chunk_copies(moves, sems, c):
            copy.wait()
        hi = jnp.clip(live - c * CHUNK, 0, CHUNK)

        @pl.when(hi > 0)
        def _():
            def half(h, _):
                decay = [row_tile(a_rows, p, h, span) for p in range(pole_count)]
                state = tuple(row_tile(z_rows, p, h, span) for p in range(pole_count))

                def step(t, state):
                    terms = list(state)
                    while len(terms) > 1:
                        terms = [x + y for x, y in zip(terms[::2], terms[1::2])]
                    y_rows[row_at(t, h, span), :] = terms[0]
                    return tuple(s * a for s, a in zip(state, decay))

                state = token_loop(jnp.int32(0), hi, step, state)
                for p in range(pole_count):
                    z_rows[row_at(p, h, span), :] = state[p]
                return 0

            lax.fori_loop(0, halves, half, 0)

        @pl.when(hi < CHUNK)
        def _():
            def zero(t, _):
                for h in range(halves):
                    y_rows[row_at(t, h, span), :] = jnp.zeros((SUBS, LANES), jnp.float32)
                return 0

            lax.fori_loop(hi, CHUNK, zero, 0)

        def block(b, _):
            rows = pl.ds(pl.multiple_of(c * CHUNK + b * 16, 16), 16)
            for j in range(tiles):
                lanes = slice(j * LANES, (j + 1) * LANES)
                y = jnp.concatenate(
                    [
                        y_rows[pl.ds((b * 16 + half * SUBS) * span + j, SUBS, stride=span), :]
                        for half in range(2)
                    ],
                    axis=0,
                )
                out_buf[rows, lanes] = (
                    q_buf[rows, lanes].astype(jnp.float32) * (w_buf[rows, lanes] + y)
                ).astype(jnp.bfloat16)
            return 0

        lax.fori_loop(0, CHUNK // 16, block, 0)
        for copy in chunk_copies(((out_buf, out_hbm),), out_sems, c):
            copy.start()
        return 0

    lax.fori_loop(0, chunks, chunk, 0)
    for c in range(chunks):
        for copy in chunk_copies(((out_buf, out_hbm),), out_sems, c):
            copy.wait()


SMEM = pl.BlockSpec(memory_space=pltpu.SMEM)
VMEM = pl.BlockSpec(memory_space=pltpu.VMEM)
ANY = pl.BlockSpec(memory_space=pl.ANY)


def params():
    return pltpu.CompilerParams(vmem_limit_bytes=VMEM_BYTES)


def swap_pairs(block, odd):
    n = lax.axis_size("ctx")
    route = [(i, (i + 1) % n if i % 2 == odd else (i - 1) % n) for i in range(n)]
    return lax.ppermute(block, "ctx", route)


def shards(q_feat, k_feat, v_feat, pole_rate, residue, skip_gain, lengths, owners):
    tok_dev, channels = q_feat.shape
    pole_count = pole_rate.shape[0]
    request_count = lengths.shape[0]
    n = lax.axis_size("ctx")
    i = lax.axis_index("ctx")
    rows = max(channels // LANES, SUBS)
    chunks = tok_dev // CHUNK
    longest = n * tok_dev // 2
    hops = max(2, -(-(longest - 1) // tok_dev))
    f32 = jnp.float32
    state_shape = jax.ShapeDtypeStruct((pole_count, channels), f32)
    far_count = n - 3
    element = tok_dev * channels * pole_count
    pieces = pl.pallas_call(
        functools.partial(pieces_kernel, request_count),
        out_shape=[state_shape] * (4 + far_count),
        in_specs=[SMEM, SMEM, ANY, ANY, VMEM],
        out_specs=[VMEM] * (4 + far_count),
        scratch_shapes=[
            pltpu.VMEM((tok_dev, channels), jnp.bfloat16),
            pltpu.VMEM((tok_dev, channels), jnp.bfloat16),
            pltpu.VMEM((CHUNK * rows, LANES), f32),
            pltpu.VMEM((pole_count * rows, LANES), f32),
            pltpu.VMEM((request_count * pole_count * rows, LANES), f32),
            pltpu.SemaphoreType.DMA((2, chunks)),
        ],
        compiler_params=params(),
        cost_estimate=pl.CostEstimate(
            flops=2 * element, bytes_accessed=4 * tok_dev * channels, transcendentals=0
        ),
        name="pieces",
    )(lengths, owners, k_feat, v_feat, pole_rate)
    even_out, odd_out, next_out, own = pieces[:4]
    is_odd = (i % 2) == 1
    even_in = swap_pairs(even_out, 0)
    odd_in = swap_pairs(odd_out, 1)
    far = [
        lax.ppermute(block, "ctx", [(j, (j + 2 + d) % n) for j in range(n)])
        for d, block in enumerate(pieces[4:])
    ]

    local = pl.pallas_call(
        functools.partial(local_kernel, request_count),
        out_shape=jax.ShapeDtypeStruct((tok_dev, channels), f32),
        in_specs=[SMEM, ANY, ANY, VMEM, VMEM, VMEM],
        out_specs=ANY,
        scratch_shapes=[
            pltpu.VMEM((tok_dev, channels), jnp.bfloat16),
            pltpu.VMEM((tok_dev, channels), jnp.bfloat16),
            pltpu.VMEM((tok_dev, channels), f32),
            pltpu.VMEM((CHUNK * rows, LANES), f32),
            pltpu.VMEM((CHUNK * rows, LANES), f32),
            pltpu.VMEM((pole_count * rows, LANES), f32),
            pltpu.VMEM((pole_count * rows, LANES), f32),
            pltpu.VMEM((pole_count * rows, LANES), f32),
            pltpu.SemaphoreType.DMA((2, chunks)),
            pltpu.SemaphoreType.DMA((1, chunks)),
        ],
        compiler_params=params(),
        cost_estimate=pl.CostEstimate(
            flops=4 * element, bytes_accessed=8 * tok_dev * channels, transcendentals=0
        ),
        name="local",
    )(lengths, k_feat, v_feat, pole_rate, residue, skip_gain[None, :])

    starts = jnp.cumsum(lengths) - lengths
    ends = starts + lengths - 1
    first = i * tok_dev
    before = jnp.sum((starts <= first - 1).astype(jnp.int32)) - 1
    behind = jnp.sum((starts <= first - tok_dev - 1).astype(jnp.int32)) - 1
    at_last = jnp.sum((starts <= first + tok_dev - 1).astype(jnp.int32)) - 1
    passing = at_last == before
    passed = (before == behind) & (before >= 0)

    from_behind = jnp.where(is_odd, even_in, odd_in)
    from_ahead = jnp.where(is_odd, odd_in, even_in)
    arrived = [from_behind]
    block = next_out
    span = jnp.exp(-pole_rate * tok_dev)
    for hop in range(1, hops):
        prior = arrived[-1] if hop == 1 else jnp.where(passed, arrived[-1], 0.0)
        block = jnp.where(passing, span * prior, next_out if hop == 1 else 0.0)
        even_hop, odd_hop = swap_pairs(block, 0), swap_pairs(block, 1)
        arrived.append(jnp.where(is_odd, even_hop, odd_hop))

    mixed_out = pl.pallas_call(
        functools.partial(finish_kernel, request_count, hops),
        out_shape=jax.ShapeDtypeStruct((tok_dev, channels), jnp.bfloat16),
        in_specs=[SMEM, ANY, ANY, VMEM, VMEM] + [VMEM] * hops,
        out_specs=ANY,
        scratch_shapes=[
            pltpu.VMEM((tok_dev, channels), f32),
            pltpu.VMEM((tok_dev, channels), jnp.bfloat16),
            pltpu.VMEM((tok_dev, channels), jnp.bfloat16),
            pltpu.VMEM((CHUNK * rows, LANES), f32),
            pltpu.VMEM((pole_count * rows, LANES), f32),
            pltpu.VMEM((pole_count * rows, LANES), f32),
            pltpu.SemaphoreType.DMA((2, chunks)),
            pltpu.SemaphoreType.DMA((1, chunks)),
        ],
        compiler_params=params(),
        cost_estimate=pl.CostEstimate(
            flops=2 * element, bytes_accessed=8 * tok_dev * channels, transcendentals=0
        ),
        name="finish",
    )(lengths, local, q_feat, pole_rate, residue, *arrived)

    owner_before = jnp.sum(jnp.where(jnp.arange(request_count) == before, owners, 0))
    end_before = jnp.sum(jnp.where(jnp.arange(request_count) == before, ends, 0))
    reach = jnp.maximum(end_before - (first - 1), 0).astype(f32)
    mine = passed & (owner_before == i)
    carried = jnp.where(mine, jnp.exp(-pole_rate * reach) * from_behind, 0.0)
    decode_state = own + from_ahead + sum(far)
    decode_state = decode_state + jnp.where(i == 0, from_behind, carried)
    decode_state = decode_state + jnp.where(passed | (i == 0), 0.0, arrived[1])
    return mixed_out, decode_state[None]


def solution(mesh):
    placed = (
        P(("groups", "ctx"), "chan"),
        P(("groups", "ctx"), "chan"),
        P(("groups", "ctx"), "chan"),
        P(None, "chan"),
        P(None, "chan"),
        P("chan"),
        P("groups"),
        P("groups"),
    )
    return jax.shard_map(
        shards,
        mesh=mesh,
        in_specs=placed,
        out_specs=(P(("groups", "ctx"), "chan"), P(("groups", "ctx"), None, "chan")),
        check_vma=False,
    )
```

```python
import functools

import jax
import jax.numpy as jnp
from jax import lax
from jax.experimental import pallas as pl
from jax.experimental.pallas import tpu as pltpu
from jax.sharding import PartitionSpec as P

LANES = 128
SUBS = 8
PACKED = 16
CHUNK = 128
UNROLL = 8
VMEM_BYTES = 28 * 1024 * 1024
F32 = jnp.float32


def request_span(lengths_ref, request, request_count):
    start = jnp.int32(0)
    length = jnp.int32(0)
    for r in range(request_count):
        start = start + jnp.where(r < request, lengths_ref[r], 0)
        length = length + jnp.where(r == request, lengths_ref[r], 0)
    return start, start + length - 1


def request_at(lengths_ref, position, request_count):
    index = jnp.int32(-1)
    start = jnp.int32(0)
    for r in range(request_count):
        index = index + (start <= position).astype(jnp.int32)
        start = start + lengths_ref[r]
    return index


def place(lengths_ref, tok_dev):
    count = lengths_ref.shape[0]
    first = lax.axis_index("ctx") * tok_dev
    before = request_at(lengths_ref, first - 1, count)
    behind = request_at(lengths_ref, first - tok_dev - 1, count)
    at_last = request_at(lengths_ref, first + tok_dev - 1, count)
    _, end = request_span(lengths_ref, before, count)
    live = jnp.where(before < 0, 0, jnp.clip(end + 1 - first, 0, tok_dev))
    passed = (before >= 0) & (before == behind)
    return before, end, live, passed, at_last


def token_loop(lo, hi, step, carry):
    count = jnp.maximum(hi - lo, 0)
    groups = lax.shift_right_logical(count, jnp.int32(UNROLL.bit_length() - 1))

    def many(g, carry):
        base = lo + g * UNROLL
        for s in range(UNROLL):
            carry = step(base + s, carry)
        return carry

    carry = lax.fori_loop(0, groups, many, carry)
    return lax.fori_loop(lo + groups * UNROLL, lo + count, step, carry)


def half_span(channels):
    tiles = channels // LANES
    return min(tiles, SUBS), max(tiles // SUBS, 1)


def state_rows(p, h, halves):
    return pl.ds(pl.multiple_of((p * halves + h) * SUBS, SUBS), SUBS)


def natural_rows(p, tile, halves):
    return pl.ds((p * halves + tile // SUBS) * SUBS + tile % SUBS, SUBS, stride=halves * SUBS)


def token_rows(t):
    return pl.ds(
        lax.shift_right_logical(t, jnp.int32(3)) * (SUBS * SUBS) + lax.bitwise_and(t, jnp.int32(7)),
        SUBS,
        stride=SUBS,
    )


def tile_rows(group, j):
    return pl.ds(pl.multiple_of((group * SUBS + j) * SUBS, SUBS), SUBS)


def each_tile(value_ref):
    pole_count, channels = value_ref.shape
    for p in range(0, pole_count, SUBS):
        for tile in range(channels // LANES):
            yield p, tile, (slice(p, p + SUBS), slice(tile * LANES, (tile + 1) * LANES))


def to_states(ref, states, change):
    _, halves = half_span(ref.shape[1])
    for p, tile, at in each_tile(ref):
        states[natural_rows(p, tile, halves), :] = change(at)


def scaled(rate_ref, residue_ref, at):
    return residue_ref[at] * jnp.sqrt(1.0 - jnp.exp(-2.0 * rate_ref[at]))


def chunk_copy(src, src_at, dst, dst_at, sem, start):
    copy = pltpu.make_async_copy(src.at[src_at], dst.at[dst_at], sem)
    if start:
        copy.start()
    else:
        copy.wait()


def token_chunk(c):
    return pl.ds(pl.multiple_of(c * CHUNK, CHUNK), CHUNK)


def fill_rows(k_buf, v_buf, u_rows, c, first_tile, width):
    def block(b, _):
        rows = pl.ds(pl.multiple_of(c * CHUNK + b * PACKED, PACKED), PACKED)
        for j in range(width):
            lanes = slice((first_tile + j) * LANES, (first_tile + j + 1) * LANES)
            u = k_buf[rows, lanes].astype(F32) * v_buf[rows, lanes].astype(F32)
            for part in range(PACKED // SUBS):
                group = c * (CHUNK // SUBS) + b * (PACKED // SUBS) + part
                u_rows[tile_rows(group, j), :] = u[part * SUBS : (part + 1) * SUBS]
        return 0

    lax.fori_loop(0, CHUNK // PACKED, block, 0)


def each_request(lengths_ref, base, extent, body):
    def request(r, start):
        length = lengths_ref[r]
        lo = jnp.maximum(start - base, 0)
        hi = jnp.minimum(start + length - base, extent)

        @pl.when(hi > lo)
        def _():
            body(r, start, lo, hi)

        return start + length

    lax.fori_loop(0, lengths_ref.shape[0], request, jnp.int32(0))


def total(terms):
    while len(terms) > 1:
        terms = [x + y for x, y in zip(terms[::2], terms[1::2])] + terms[len(terms) // 2 * 2 :]
    return terms[0]


def pieces_kernel(lengths_hbm, owners_hbm, k_hbm, v_hbm, rate_hbm, residue_hbm, *rest):
    n = lax.axis_size("ctx")
    i = lax.axis_index("ctx")
    far_count = n - 2
    even_ref, odd_ref, next_ref, own_ref = rest[:4]
    far_refs = rest[4 : 4 + far_count]
    u_rows, decays, gains = rest[4 + far_count : 7 + far_count]
    (
        k_buf, v_buf, rate_ref, residue_ref, lengths_ref, owners_ref, states, sems, small_sems,
    ) = rest[7 + far_count :]
    request_count = lengths_ref.shape[0]
    pole_count, channels = rate_ref.shape
    tok_dev = k_buf.shape[0]
    width, halves = half_span(channels)
    chunks = tok_dev // CHUNK
    first = i * tok_dev
    last = first + tok_dev - 1

    def moves(c, start):
        rows = (token_chunk(c), slice(None))
        chunk_copy(k_hbm, rows, k_buf, rows, sems.at[0, c], start)
        chunk_copy(v_hbm, rows, v_buf, rows, sems.at[1, c], start)

    small = [
        pltpu.make_async_copy(src, dst, small_sems.at[n])
        for n, (src, dst) in enumerate(
            (
                (lengths_hbm, lengths_ref),
                (owners_hbm, owners_ref),
                (rate_hbm, rate_ref),
                (residue_hbm, residue_ref),
            )
        )
    ]
    for copy in small:
        copy.start()
    for c in range(chunks):
        moves(c, True)

    def clear(b, _):
        states[pl.ds(pl.multiple_of(b * SUBS, SUBS), SUBS), :] = jnp.zeros((SUBS, LANES), F32)
        return 0

    lax.fori_loop(0, request_count * pole_count * halves, clear, 0)
    for copy in small:
        copy.wait()
    to_states(rate_ref, decays, lambda at: jnp.exp(-rate_ref[at]))
    to_states(rate_ref, gains, lambda at: scaled(rate_ref, residue_ref, at))

    def chunk(c, _):
        moves(c, False)
        for h in range(halves):
            fill_rows(k_buf, v_buf, u_rows.at[h], c, h * SUBS, width)
        base = c * CHUNK

        def request(r, start, lo, hi):
            def half(h, _):
                decay = [decays[state_rows(p, h, halves), :] for p in range(pole_count)]
                row = r * pole_count
                state = tuple(
                    states[state_rows(row + p, h, halves), :] for p in range(pole_count)
                )

                def step(t, state):
                    u = u_rows[h, token_rows(t), :]
                    return tuple(s * a + u for s, a in zip(state, decay))

                state = token_loop(base + lo, base + hi, step, state)
                for p in range(pole_count):
                    states[state_rows(row + p, h, halves), :] = state[p]
                return 0

            lax.fori_loop(0, halves, half, 0)

        each_request(lengths_ref, first + c * CHUNK, CHUNK, request)
        return 0

    lax.fori_loop(0, chunks, chunk, 0)

    def owned(slot):
        request = jnp.int32(0)
        found = jnp.int32(0)
        for r in range(request_count):
            match = (owners_ref[r] == slot).astype(jnp.int32)
            request = request + r * match
            found = found + match
        start, end = request_span(lengths_ref, request, request_count)
        live = (found > 0) & (start <= last) & (end >= first)
        return request, jnp.maximum(end - last, 0), live

    def emit(out_ref, what):
        request, steps, live = what
        back = -steps.astype(F32)
        keep = jnp.where(live, 1.0, 0.0).astype(F32)
        for p, tile, at in each_tile(rate_ref):
            state = states[natural_rows(request * pole_count + p, tile, halves), :]
            out_ref[at] = state * (jnp.exp(rate_ref[at] * back) * keep)

    def pick(flag, yes, no):
        return tuple(jnp.where(flag, a, b) for a, b in zip(yes, no))

    odd = lax.rem(i, 2) == 1
    crossing = (request_at(lengths_ref, last, request_count), jnp.int32(0), jnp.bool_(True))
    behind = owned(i - 1)
    ahead = owned(i + 1)
    emit(even_ref, pick(odd, behind, crossing))
    emit(odd_ref, pick(odd, crossing, behind))
    for d, far_ref in enumerate(far_refs[:-1]):
        emit(far_ref, owned(lax.rem(i + 2 + d, n)))
    emit(far_refs[-1], owned(n - 1 - i))
    emit(next_ref, ahead)
    emit(own_ref, owned(i))


def forward_in(even_ref, odd_ref, at):
    odd = lax.rem(lax.axis_index("ctx"), 2) == 1
    return jnp.where(odd, even_ref[at], odd_ref[at])


def relay_kernel(tok_dev, lengths_ref, rate_ref, even_ref, odd_ref, next_ref, out_ref):
    before, _, _, _, at_last = place(lengths_ref, tok_dev)
    passing = (before >= 0) & (before == at_last)
    for _, _, at in each_tile(rate_ref):
        moved = jnp.exp(rate_ref[at] * -float(tok_dev)) * forward_in(even_ref, odd_ref, at)
        out_ref[at] = jnp.where(passing, moved, next_ref[at])


def later_relay_kernel(tok_dev, lengths_ref, rate_ref, even_ref, odd_ref, out_ref):
    before, _, _, passed, at_last = place(lengths_ref, tok_dev)
    passing = passed & (before == at_last)
    for _, _, at in each_tile(rate_ref):
        moved = jnp.exp(rate_ref[at] * -float(tok_dev)) * forward_in(even_ref, odd_ref, at)
        out_ref[at] = jnp.where(passing, moved, 0.0)


def conv_half(lengths_ref, decay, gain, skip, begin, states, u_rows, y_rows, tok_dev):
    pole_count = len(decay)
    first = lax.axis_index("ctx") * tok_dev
    for p in range(pole_count):
        states[state_rows(p, 0, 1), :] = begin[p]

    def request(r, start, lo, hi):
        fresh = start >= first
        state = tuple(
            jnp.where(fresh, 0.0, states[state_rows(p, 0, 1), :]) for p in range(pole_count)
        )

        def step(t, state):
            u = u_rows[token_rows(t), :]
            state = tuple(s * a + u for s, a in zip(state, decay))
            y_rows[token_rows(t), :] = total([s * g for s, g in zip(state, gain)] + [skip * u])
            return state

        token_loop(lo, hi, step, state)

    each_request(lengths_ref, first, tok_dev, request)


def correct_half(decay, state, w_rows, y_rows, lo, hi):
    def step(t, state):
        rows = token_rows(t)
        y_rows[rows, :] = w_rows[rows, :] + total(list(state))
        return tuple(s * a for s, a in zip(state, decay))

    return token_loop(lo, hi, step, state)


def local_kernel(lengths_ref, u_rows, decays, gains, skip_ref, w_rows, states):
    tok_dev = w_rows.shape[0] // SUBS
    halves = u_rows.shape[0]
    pole_count = decays.shape[0] // (halves * SUBS)
    decay = [decays[state_rows(p, 0, halves), :] for p in range(pole_count)]
    gain = [gains[state_rows(p, 0, halves), :] for p in range(pole_count)]
    zero = [jnp.zeros((SUBS, LANES), F32)] * pole_count
    conv_half(
        lengths_ref, decay, gain, skip_ref[0:SUBS, :], zero, states, u_rows.at[0], w_rows, tok_dev
    )


def joined_kernel(
    lengths_ref, u_rows, decays, gains, skip_ref, even_ref, odd_ref, w_rows, _, y_rows,
    incoming, states,
):
    tok_dev = w_rows.shape[0] // SUBS
    halves = u_rows.shape[0]
    pole_count = even_ref.shape[0]
    before, _, live, _, _ = place(lengths_ref, tok_dev)
    to_states(
        even_ref, incoming, lambda at: jnp.where(before < 0, 0.0, forward_in(even_ref, odd_ref, at))
    )
    decay = [decays[state_rows(p, 0, halves), :] for p in range(pole_count)]
    state = tuple(
        incoming[state_rows(p, 0, halves), :] * decay[p] * gains[state_rows(p, 0, halves), :]
        for p in range(pole_count)
    )
    correct_half(decay, state, w_rows, y_rows.at[0], jnp.int32(0), live)

    def keep(t, _):
        rows = token_rows(t)
        y_rows[0, rows, :] = w_rows[rows, :]
        return 0

    token_loop(live, jnp.int32(tok_dev), keep, 0)
    for h in range(1, halves):
        decay = [decays[state_rows(p, h, halves), :] for p in range(pole_count)]
        gain = [gains[state_rows(p, h, halves), :] for p in range(pole_count)]
        begin = [incoming[state_rows(p, h, halves), :] for p in range(pole_count)]
        conv_half(
            lengths_ref, decay, gain, skip_ref[h * SUBS : (h + 1) * SUBS, :], begin, states,
            u_rows.at[h], y_rows.at[h], tok_dev,
        )


def finish_kernel(later_count, lengths_ref, w_rows, q_hbm, decays, gains, *rest):
    later_refs = rest[: 2 * later_count]
    out_hbm, q_buf, out_buf, y_rows, spread, fading, sems, out_sems = rest[2 * later_count :]
    tok_dev = q_buf.shape[0]
    halves = w_rows.shape[0]
    pole_count, channels = later_refs[0].shape
    width, _ = half_span(channels)
    chunks = tok_dev // CHUNK
    _, _, live, passed, _ = place(lengths_ref, tok_dev)
    live = jnp.where(passed, live, 0)

    def moves(c, start):
        rows = (token_chunk(c), slice(None))
        chunk_copy(q_hbm, rows, q_buf, rows, sems.at[c], start)

    def results(c, start):
        rows = (token_chunk(c), slice(None))
        chunk_copy(out_buf, rows, out_hbm, rows, out_sems.at[c], start)

    for c in range(chunks):
        moves(c, True)

    @pl.when(live > 0)
    def _():
        def begin(at):
            state = forward_in(later_refs[0], later_refs[1], at)
            for hop in range(1, later_count):
                state = state + forward_in(later_refs[2 * hop], later_refs[2 * hop + 1], at)
            return state

        to_states(later_refs[0], spread, begin)
        for p in range(pole_count):
            for h in range(halves):
                at = state_rows(p, h, halves)
                fading[h, state_rows(p, 0, 1), :] = spread[at, :] * gains[at, :] * decays[at, :]

    def gate(rows_ref, c):
        def block(b, _):
            rows = pl.ds(pl.multiple_of(c * CHUNK + b * PACKED, PACKED), PACKED)
            group = (c * CHUNK + b * PACKED) // SUBS
            for h in range(halves):
                for j in range(width):
                    lanes = slice((h * SUBS + j) * LANES, (h * SUBS + j + 1) * LANES)
                    w = jnp.concatenate(
                        [
                            rows_ref[h, tile_rows(group + part, j), :]
                            for part in range(PACKED // SUBS)
                        ],
                        axis=0,
                    )
                    out_buf[rows, lanes] = (q_buf[rows, lanes].astype(F32) * w).astype(jnp.bfloat16)
            return 0

        lax.fori_loop(0, CHUNK // PACKED, block, 0)

    def chunk(c, _):
        moves(c, False)
        lo = c * CHUNK
        hi = jnp.clip(live, lo, lo + CHUNK)

        @pl.when(hi > lo)
        def _():
            def half(h, _):
                decay = [decays[state_rows(p, h, halves), :] for p in range(pole_count)]
                state = tuple(fading[h, state_rows(p, 0, 1), :] for p in range(pole_count))
                w, y = w_rows.at[h], y_rows.at[h]
                state = correct_half(decay, state, w, y, lo, hi)
                for p in range(pole_count):
                    fading[h, state_rows(p, 0, 1), :] = state[p]

                def keep(t, _):
                    y[token_rows(t), :] = w[token_rows(t), :]
                    return 0

                token_loop(hi, lo + CHUNK, keep, 0)
                return 0

            lax.fori_loop(0, halves, half, 0)
            gate(y_rows, c)

        @pl.when(hi == lo)
        def _():
            gate(w_rows, c)

        results(c, True)
        return 0

    lax.fori_loop(0, chunks, chunk, 0)
    for c in range(chunks):
        results(c, False)


def gather_kernel(
    tok_dev, lengths_ref, owners_ref, rate_ref, own_ref, even_ref, odd_ref, even_next_ref,
    odd_next_ref, *rest,
):
    far_refs, out_ref = rest[:-1], rest[-1]
    n = lax.axis_size("ctx")
    i = lax.axis_index("ctx")
    before, end, _, passed, _ = place(lengths_ref, tok_dev)
    owner = jnp.int32(-1)
    for r in range(lengths_ref.shape[0]):
        owner = jnp.where(r == before, owners_ref[r], owner)
    mine = passed & (owner == i)
    back = -jnp.maximum(end - (i * tok_dev - 1), 0).astype(F32)
    odd = lax.rem(i, 2) == 1
    end_device = (i == 0) | (i == n - 1)
    for _, _, at in each_tile(rate_ref):
        value = own_ref[at]
        for ref in far_refs[:-1]:
            value = value + ref[at]
        value = value + jnp.where(end_device, far_refs[-1][at], 0.0)
        ahead = jnp.where(odd, odd_ref[at], even_ref[at])
        value = value + jnp.where(i == n - 1, 0.0, ahead)
        slot = forward_in(even_next_ref, odd_next_ref, at)
        value = value + jnp.where(passed | (i == 0), 0.0, slot)
        crossing = forward_in(even_ref, odd_ref, at) * jnp.exp(rate_ref[at] * back)
        out_ref[0, at[0], at[1]] = value + jnp.where(mine, crossing, 0.0)


SMEM = pl.BlockSpec(memory_space=pltpu.SMEM)
VMEM = pl.BlockSpec(memory_space=pltpu.VMEM)
HBM = pl.BlockSpec(memory_space=pltpu.HBM)
DMA = pltpu.SemaphoreType.DMA


def in_hbm(x):
    return pltpu.with_memory_space_constraint(x, pltpu.HBM)


def call(kernel, name, out_shape, in_specs, out_specs, scratch=(), cost=(0, 0), aliases=None):
    return pl.pallas_call(
        kernel,
        out_shape=out_shape,
        in_specs=in_specs,
        out_specs=out_specs,
        scratch_shapes=list(scratch),
        compiler_params=pltpu.CompilerParams(vmem_limit_bytes=VMEM_BYTES),
        cost_estimate=pl.CostEstimate(flops=cost[0], bytes_accessed=cost[1], transcendentals=0),
        input_output_aliases=aliases or {},
        name=name,
    )


def swap(block, partner):
    n, lanes = lax.axis_size("ctx"), lax.axis_size("chan")
    route = []
    for i in range(n):
        for c in range(lanes):
            j = partner(i)
            to = j * lanes + c if j is not None else i * lanes + (c ^ 1)
            route.append((i * lanes + c, to))
    return lax.ppermute(block, ("ctx", "chan"), route)


def shards(q_feat, k_feat, v_feat, pole_rate, residue, skip_gain, lengths, owners):
    tok_dev, channels = q_feat.shape
    pole_count = pole_rate.shape[0]
    request_count = lengths.shape[0]
    n = lax.axis_size("ctx")
    width, halves = half_span(channels)
    chunks = tok_dev // CHUNK
    longest = n * tok_dev // 2
    hops = max(2, -(-(longest - 1) // tok_dev))
    state_shape = jax.ShapeDtypeStruct((pole_count, channels), F32)
    rows_shape = jax.ShapeDtypeStruct((tok_dev * SUBS, LANES), F32)
    far_count = n - 2
    element = tok_dev * channels * pole_count
    token_bytes = tok_dev * channels
    half_state = pltpu.VMEM((pole_count * SUBS, LANES), F32)
    state_rows_shape = jax.ShapeDtypeStruct((pole_count * halves * SUBS, LANES), F32)
    state = pltpu.VMEM(state_rows_shape.shape, F32)
    all_rows = jax.ShapeDtypeStruct((halves, tok_dev * SUBS, LANES), F32)

    pieces = call(
        pieces_kernel,
        "pieces",
        [state_shape] * (4 + far_count) + [all_rows, state_rows_shape, state_rows_shape],
        [HBM] * 6,
        [VMEM] * (7 + far_count),
        [
            pltpu.VMEM((tok_dev, channels), jnp.bfloat16),
            pltpu.VMEM((tok_dev, channels), jnp.bfloat16),
            pltpu.VMEM((pole_count, channels), F32),
            pltpu.VMEM((pole_count, channels), F32),
            pltpu.SMEM((request_count,), jnp.int32),
            pltpu.SMEM((request_count,), jnp.int32),
            pltpu.VMEM((request_count * pole_count * halves * SUBS, LANES), F32),
            DMA((2, chunks)),
            DMA((4,)),
        ],
        (2 * element, 8 * token_bytes),
    )(*map(in_hbm, (lengths, owners, k_feat, v_feat, pole_rate, residue)))
    u_rows, decays, gains = pieces[-3:]
    even_out, odd_out, next_out, own = pieces[:4]
    far_out = pieces[4:-3]

    def even_partner(i):
        return i ^ 1

    def odd_partner(i):
        j = i + 1 if i % 2 else i - 1
        return j if 0 <= j < n else None

    even_in = swap(even_out, even_partner)
    odd_in = swap(odd_out, odd_partner)

    skip_rows = skip_gain.reshape(-1, LANES)
    if skip_rows.shape[0] < SUBS:
        skip_rows = jnp.pad(skip_rows, ((0, SUBS - skip_rows.shape[0]), (0, 0)))

    half_local = call(
        local_kernel,
        "local",
        rows_shape,
        [SMEM] + [VMEM] * 4,
        VMEM,
        [half_state],
        (4 * element // halves, 8 * token_bytes // halves),
    )(lengths, u_rows, decays, gains, skip_rows)

    even_in, odd_in, half_local = lax.optimization_barrier((even_in, odd_in, half_local))
    relayed = call(
        functools.partial(relay_kernel, tok_dev),
        "relay",
        state_shape,
        [SMEM, VMEM, VMEM, VMEM, VMEM],
        VMEM,
    )(lengths, pole_rate, even_in, odd_in, next_out)
    later = [swap(relayed, even_partner), swap(relayed, odd_partner)]
    far_in = [
        lax.ppermute(block, "ctx", [(j, (j + 2 + d) % n) for j in range(n)])
        for d, block in enumerate(far_out[:-1])
    ]
    far_in.append(swap(far_out[-1], lambda i: n - 1 - i if i in (0, n - 1) else None))

    joined = call(
        joined_kernel,
        "joined",
        all_rows,
        [SMEM] + [VMEM] * 8,
        VMEM,
        [state, half_state],
        (4 * element, 16 * token_bytes),
    )(lengths, u_rows, decays, gains, skip_rows, even_in, odd_in, half_local, relayed)

    for _ in range(2, hops):
        block = call(
            functools.partial(later_relay_kernel, tok_dev),
            "relay",
            state_shape,
            [SMEM, VMEM, VMEM, VMEM],
            VMEM,
        )(lengths, pole_rate, later[-2], later[-1])
        later += [swap(block, even_partner), swap(block, odd_partner)]

    mixed_out = call(
        functools.partial(finish_kernel, hops - 1),
        "finish",
        jax.ShapeDtypeStruct((tok_dev, channels), jnp.bfloat16),
        [SMEM, VMEM, HBM, VMEM, VMEM] + [VMEM] * len(later),
        HBM,
        [
            pltpu.VMEM((tok_dev, channels), jnp.bfloat16),
            pltpu.VMEM((tok_dev, channels), jnp.bfloat16),
            pltpu.VMEM(all_rows.shape, F32),
            state,
            pltpu.VMEM((halves, pole_count * SUBS, LANES), F32),
            DMA((chunks,)),
            DMA((chunks,)),
        ],
        (2 * element, 8 * token_bytes),
    )(lengths, joined, q_feat, decays, gains, *later)

    decode_state = call(
        functools.partial(gather_kernel, tok_dev),
        "gather",
        jax.ShapeDtypeStruct((1, pole_count, channels), F32),
        [SMEM, SMEM] + [VMEM] * (6 + far_count),
        VMEM,
    )(lengths, owners, pole_rate, own, even_in, odd_in, later[0], later[1], *far_in)
    return mixed_out, decode_state


def solution(mesh):
    placed = (
        P(("groups", "ctx"), "chan"),
        P(("groups", "ctx"), "chan"),
        P(("groups", "ctx"), "chan"),
        P(None, "chan"),
        P(None, "chan"),
        P("chan"),
        P("groups"),
        P("groups"),
    )
    return jax.shard_map(
        shards,
        mesh=mesh,
        in_specs=placed,
        out_specs=(P(("groups", "ctx"), "chan"), P(("groups", "ctx"), None, "chan")),
        check_vma=False,
    )
```

```python
import functools

import jax
import jax.numpy as jnp
from jax import lax
from jax.experimental import pallas as pl
from jax.experimental.pallas import tpu as pltpu
from jax.sharding import PartitionSpec as P

LANES = 128
SUBS = 8
PACKED = 16
CHUNK = 128
BLOCK = 16
UNROLL = 8
VMEM_BYTES = 28 * 1024 * 1024
F32 = jnp.float32


def request_span(lengths_ref, request, request_count):
    start = jnp.int32(0)
    length = jnp.int32(0)
    for r in range(request_count):
        start = start + jnp.where(r < request, lengths_ref[r], 0)
        length = length + jnp.where(r == request, lengths_ref[r], 0)
    return start, start + length - 1


def request_at(lengths_ref, position, request_count):
    index = jnp.int32(-1)
    start = jnp.int32(0)
    for r in range(request_count):
        index = index + (start <= position).astype(jnp.int32)
        start = start + lengths_ref[r]
    return index


def request_before(lengths_ref, tok_dev, hop):
    first = lax.axis_index("ctx") * tok_dev
    return request_at(lengths_ref, first - (hop - 1) * tok_dev - 1, lengths_ref.shape[0])


def token_loop(lo, hi, step, carry):
    count = jnp.maximum(hi - lo, 0)
    groups = lax.shift_right_logical(count, jnp.int32(UNROLL.bit_length() - 1))

    def many(g, carry):
        base = lo + g * UNROLL
        for s in range(UNROLL):
            carry = step(base + s, carry)
        return carry

    carry = lax.fori_loop(0, groups, many, carry)
    return lax.fori_loop(lo + groups * UNROLL, lo + count, step, carry)


def half_span(channels):
    tiles = channels // LANES
    return min(tiles, SUBS), max(tiles // SUBS, 1)


def state_rows(p, h, halves):
    return pl.ds(pl.multiple_of((p * halves + h) * SUBS, SUBS), SUBS)


def natural_rows(p, tile, halves):
    return pl.ds((p * halves + tile // SUBS) * SUBS + tile % SUBS, SUBS, stride=halves * SUBS)


def token_rows(t):
    return pl.ds(
        lax.shift_right_logical(t, jnp.int32(3)) * (SUBS * SUBS) + lax.bitwise_and(t, jnp.int32(7)),
        SUBS,
        stride=SUBS,
    )


def block_token(b, s):
    return pl.ds(b * (BLOCK * SUBS) + s // SUBS * (SUBS * SUBS) + s % SUBS, SUBS, stride=SUBS)


def saved_rows(b, p, pole_count):
    return pl.ds(pl.multiple_of((b * pole_count + p) * SUBS, SUBS), SUBS)


def block_parts(lo, hi):
    head = jnp.minimum(hi, lax.bitwise_and(lo + (BLOCK - 1), jnp.int32(-BLOCK)))
    shift = jnp.int32(BLOCK.bit_length() - 1)
    first = lax.shift_right_logical(head + (BLOCK - 1), shift)
    last = jnp.maximum(lax.shift_right_logical(hi, shift), first)
    return head, first, last, jnp.maximum(last * BLOCK, head)


def tile_rows(group, j):
    return pl.ds(pl.multiple_of((group * SUBS + j) * SUBS, SUBS), SUBS)


def each_tile(value_ref):
    pole_count, channels = value_ref.shape
    for p in range(0, pole_count, SUBS):
        for tile in range(channels // LANES):
            yield p, tile, (slice(p, p + SUBS), slice(tile * LANES, (tile + 1) * LANES))


def to_states(ref, states, change):
    _, halves = half_span(ref.shape[1])
    for p, tile, at in each_tile(ref):
        states[natural_rows(p, tile, halves), :] = change(at)


def scaled(rate_ref, residue_ref, at):
    return residue_ref[at] * jnp.sqrt(1.0 - jnp.exp(-2.0 * rate_ref[at]))


def chunk_copy(src, src_at, dst, dst_at, sem, start):
    copy = pltpu.make_async_copy(src.at[src_at], dst.at[dst_at], sem)
    if start:
        copy.start()
    else:
        copy.wait()


def token_chunk(c):
    return pl.ds(pl.multiple_of(c * CHUNK, CHUNK), CHUNK)


def fill_rows(k_buf, v_buf, u_rows, c, first_tile, width):
    def block(b, _):
        rows = pl.ds(pl.multiple_of(c * CHUNK + b * PACKED, PACKED), PACKED)
        for j in range(width):
            lanes = slice((first_tile + j) * LANES, (first_tile + j + 1) * LANES)
            u = k_buf[rows, lanes].astype(F32) * v_buf[rows, lanes].astype(F32)
            for part in range(PACKED // SUBS):
                group = c * (CHUNK // SUBS) + b * (PACKED // SUBS) + part
                u_rows[tile_rows(group, j), :] = u[part * SUBS : (part + 1) * SUBS]
        return 0

    lax.fori_loop(0, CHUNK // PACKED, block, 0)


def each_request(lengths_ref, base, extent, body):
    def request(r, start):
        length = lengths_ref[r]
        lo = jnp.maximum(start - base, 0)
        hi = jnp.minimum(start + length - base, extent)

        @pl.when(hi > lo)
        def _():
            body(r, start, lo, hi)

        return start + length

    lax.fori_loop(0, lengths_ref.shape[0], request, jnp.int32(0))


def total(terms):
    while len(terms) > 1:
        terms = [x + y for x, y in zip(terms[::2], terms[1::2])] + terms[len(terms) // 2 * 2 :]
    return terms[0]


def pieces_kernel(
    lengths_hbm, owners_hbm, k_hbm, v_hbm, rate_hbm, residue_hbm,
    cross_ref, pair_ref, mine_ref, u_rows, decays, gains, saved,
    k_buf, v_buf, rate_ref, residue_ref, lengths_ref, owners_ref, states, sems, small_sems,
):
    n = lax.axis_size("ctx")
    i = lax.axis_index("ctx")
    request_count = lengths_ref.shape[0]
    pole_count, channels = rate_ref.shape
    tok_dev = k_buf.shape[0]
    width, halves = half_span(channels)
    chunks = tok_dev // CHUNK
    first = i * tok_dev
    last = first + tok_dev - 1

    def moves(c, start):
        rows = (token_chunk(c), slice(None))
        chunk_copy(k_hbm, rows, k_buf, rows, sems.at[0, c], start)
        chunk_copy(v_hbm, rows, v_buf, rows, sems.at[1, c], start)

    small = [
        pltpu.make_async_copy(src, dst, small_sems.at[n])
        for n, (src, dst) in enumerate(
            (
                (lengths_hbm, lengths_ref),
                (owners_hbm, owners_ref),
                (rate_hbm, rate_ref),
                (residue_hbm, residue_ref),
            )
        )
    ]
    for copy in small:
        copy.start()
    for c in range(chunks):
        moves(c, True)

    def clear(b, _):
        states[pl.ds(pl.multiple_of(b * SUBS, SUBS), SUBS), :] = jnp.zeros((SUBS, LANES), F32)
        return 0

    lax.fori_loop(0, request_count * pole_count * halves, clear, 0)
    for copy in small:
        copy.wait()
    to_states(rate_ref, decays, lambda at: jnp.exp(-rate_ref[at]))
    to_states(rate_ref, gains, lambda at: scaled(rate_ref, residue_ref, at))

    def chunk(c, _):
        moves(c, False)
        for h in range(halves):
            fill_rows(k_buf, v_buf, u_rows.at[h], c, h * SUBS, width)
        base = c * CHUNK

        def request(r, start, lo, hi):
            head, begin, end, tail = block_parts(base + lo, base + hi)

            def half(h, _):
                decay = [decays[state_rows(p, h, halves), :] for p in range(pole_count)]
                row = r * pole_count
                state = tuple(
                    states[state_rows(row + p, h, halves), :] for p in range(pole_count)
                )

                def advance(state, u):
                    return tuple(s * a + u for s, a in zip(state, decay))

                def single(t, state):
                    return advance(state, u_rows[h, token_rows(t), :])

                def save(b, state):
                    for p in range(pole_count):
                        saved[h, saved_rows(b, p, pole_count), :] = state[p]

                def block(b, state):
                    save(b, state)
                    for s in range(BLOCK):
                        state = advance(state, u_rows[h, block_token(b, s), :])
                    return state

                state = lax.fori_loop(base + lo, head, single, state)
                state = lax.fori_loop(begin, end, block, state)

                @pl.when(base + hi > tail)
                def _():
                    save(end, state)

                state = lax.fori_loop(tail, base + hi, single, state)
                for p in range(pole_count):
                    states[state_rows(row + p, h, halves), :] = state[p]
                return 0

            lax.fori_loop(0, halves, half, 0)

        each_request(lengths_ref, first + base, CHUNK, request)
        return 0

    lax.fori_loop(0, chunks, chunk, 0)

    def emit(out_ref, m, slot):
        request = jnp.int32(0)
        found = jnp.int32(0)
        for r in range(request_count):
            match = (owners_ref[r] == slot).astype(jnp.int32)
            request = request + r * match
            found = found + match
        start, end = request_span(lengths_ref, request, request_count)
        live = (found > 0) & (start <= last) & (end >= first)
        back = -jnp.maximum(end - last, 0).astype(F32)
        keep = jnp.where(live, 1.0, 0.0).astype(F32)
        for p, tile, at in each_tile(rate_ref):
            state = states[natural_rows(request * pole_count + p, tile, halves), :]
            out_ref[m, at[0], at[1]] = state * (jnp.exp(rate_ref[at] * back) * keep)

    crossing = request_at(lengths_ref, last, request_count)
    for p, tile, at in each_tile(rate_ref):
        state = states[natural_rows(crossing * pole_count + p, tile, halves), :]
        cross_ref[at] = state
        pair_ref[0, at[0], at[1]] = state
    odd = lax.rem(i, 2)
    for m in range(n // 2):
        emit(pair_ref, 1 + m, 2 * m + 1 - odd)
        emit(mine_ref, m, 2 * m + odd)


def taps_kernel(lengths_ref, u_rows, decays, gains, skip_ref, y_rows, taps):
    halves = u_rows.shape[0]
    tok_dev = u_rows.shape[1] // SUBS
    pole_count = decays.shape[0] // (halves * SUBS)
    first = lax.axis_index("ctx") * tok_dev

    def half(h, _):
        skip = skip_ref[pl.ds(pl.multiple_of(h * SUBS, SUBS), SUBS), :]
        decay = [decays[state_rows(p, h, halves), :] for p in range(pole_count)]
        power = [gains[state_rows(p, h, halves), :] for p in range(pole_count)]
        for j in range(BLOCK):
            tap = total(list(power))
            taps[j * SUBS : (j + 1) * SUBS, :] = tap + skip if j == 0 else tap
            power = [x * a for x, a in zip(power, decay)]

        def request(r, start, lo, hi):
            head, begin, end, tail = block_parts(lo, hi)

            def alone(lo, hi):
                decay = [decays[state_rows(p, h, halves), :] for p in range(pole_count)]
                gain = [gains[state_rows(p, h, halves), :] for p in range(pole_count)]

                def single(t, state):
                    u = u_rows[h, token_rows(t), :]
                    state = tuple(s * a + u for s, a in zip(state, decay))
                    y_rows[h, token_rows(t), :] = total(
                        [s * g for s, g in zip(state, gain)] + [skip * u]
                    )
                    return state

                zero = jnp.zeros((SUBS, LANES), F32)
                lax.fori_loop(lo, hi, single, (zero,) * pole_count)

            @pl.when(head > lo)
            def _():
                alone(lo, head)

            @pl.when(hi > tail)
            def _():
                alone(tail, hi)

            tap = [taps[j * SUBS : (j + 1) * SUBS, :] for j in range(BLOCK)]

            def block(b, _):
                u = [u_rows[h, block_token(b, s), :] for s in range(BLOCK)]
                for s in range(BLOCK):
                    y_rows[h, block_token(b, s), :] = total(
                        [tap[j] * u[s - j] for j in range(s + 1)]
                    )
                return 0

            lax.fori_loop(begin, end, block, 0)

        each_request(lengths_ref, first, tok_dev, request)
        return 0

    lax.fori_loop(0, halves, half, 0)


def pool_kernel(mine_ref, pair_ref, *rest):
    n = lax.axis_size("ctx")
    i = lax.axis_index("ctx")
    keep_ref, far_refs = rest[0], rest[1:]
    for d, ref in enumerate((keep_ref,) + far_refs):
        m = lax.div(lax.rem(i + 2 * d, n), 2)
        for _, _, at in each_tile(keep_ref):
            ref[at] = mine_ref[m, at[0], at[1]] + pair_ref[1 + m, at[0], at[1]]


def finish_kernel(
    skip_count, lengths_ref, y_rows, saved, q_hbm, decays, gains, rate_ref, pair_ref, odd_ref, *rest
):
    skip_refs = rest[:skip_count]
    out_hbm, q_buf, out_buf, w_rows, spread, fading, sems, out_sems = rest[skip_count:]
    i = lax.axis_index("ctx")
    tok_dev = q_buf.shape[0]
    halves = y_rows.shape[0]
    pole_count, channels = rate_ref.shape
    width, _ = half_span(channels)
    chunks = tok_dev // CHUNK
    first = i * tok_dev
    before = request_before(lengths_ref, tok_dev, 1)

    def moves(c, start):
        rows = (token_chunk(c), slice(None))
        chunk_copy(q_hbm, rows, q_buf, rows, sems.at[c], start)

    def results(c, start):
        rows = (token_chunk(c), slice(None))
        chunk_copy(out_buf, rows, out_hbm, rows, out_sems.at[c], start)

    for c in range(chunks):
        moves(c, True)
    odd = lax.rem(i, 2) == 1
    reached = [
        (before >= 0) & (request_before(lengths_ref, tok_dev, hop) == before)
        for hop in range(1, skip_count + 2)
    ]

    def incoming(at):
        state = jnp.where(odd, pair_ref[0, at[0], at[1]], odd_ref[at])
        state = jnp.where(reached[0], state, 0.0)
        for hop, ref in enumerate(skip_refs, 1):
            moved = ref[at] * jnp.exp(rate_ref[at] * -float(hop * tok_dev))
            state = state + jnp.where(reached[hop], moved, 0.0)
        return state

    to_states(rate_ref, spread, incoming)
    for p in range(pole_count):
        for h in range(halves):
            at = state_rows(p, h, halves)
            fading[h, state_rows(p, 0, 1), :] = spread[at, :] * gains[at, :] * decays[at, :]

    def gate(c):
        def block(b, _):
            rows = pl.ds(pl.multiple_of(c * CHUNK + b * PACKED, PACKED), PACKED)
            for h in range(halves):
                for j in range(width):
                    lanes = slice((h * SUBS + j) * LANES, (h * SUBS + j + 1) * LANES)
                    w = jnp.concatenate(
                        [
                            w_rows[h, tile_rows(b * (PACKED // SUBS) + part, j), :]
                            for part in range(PACKED // SUBS)
                        ],
                        axis=0,
                    )
                    out_buf[rows, lanes] = (q_buf[rows, lanes].astype(F32) * w).astype(jnp.bfloat16)
            return 0

        lax.fori_loop(0, CHUNK // PACKED, block, 0)

    def chunk(c, _):
        moves(c, False)
        base = c * CHUNK

        def request(r, start, lo, hi):
            head, begin, end, tail = block_parts(lo, hi)

            def half(h, _):
                y = y_rows.at[h, pl.ds(pl.multiple_of(base * SUBS, CHUNK * SUBS), CHUNK * SUBS)]
                w = w_rows.at[h]

                @pl.when(start >= first)
                def _():
                    fading[h] = jnp.zeros(fading.shape[1:], F32)

                def keep(t, _):
                    w[token_rows(t), :] = y[token_rows(t), :]
                    return 0

                lax.fori_loop(lo, head, keep, 0)
                decay = [decays[state_rows(p, h, halves), :] for p in range(pole_count)]

                def opening(b):
                    state = []
                    for p in range(pole_count):
                        at = state_rows(p, h, halves)
                        local = saved[h, saved_rows(base // BLOCK + b, p, pole_count), :]
                        state.append(
                            local * (gains[at, :] * decays[at, :])
                            + fading[h, state_rows(p, 0, 1), :]
                        )
                    return state

                def block(b, _):
                    state = opening(b)
                    for p in range(pole_count):
                        at = state_rows(p, 0, 1)
                        power = decay[p]
                        for _ in range(BLOCK.bit_length() - 1):
                            power = power * power
                        fading[h, at, :] = fading[h, at, :] * power
                    for s in range(BLOCK):
                        rows = block_token(b, s)
                        w[rows, :] = y[rows, :] + total(list(state))
                        if s < BLOCK - 1:
                            state = [x * a for x, a in zip(state, decay)]
                    return 0

                lax.fori_loop(begin, end, block, 0)

                @pl.when(hi > tail)
                def _():
                    def single(t, state):
                        w[token_rows(t), :] = y[token_rows(t), :] + total(list(state))
                        return tuple(x * a for x, a in zip(state, decay))

                    lax.fori_loop(tail, hi, single, tuple(opening(end)))

                return 0

            lax.fori_loop(0, halves, half, 0)

        each_request(lengths_ref, first + base, CHUNK, request)
        gate(c)
        results(c, True)
        return 0

    lax.fori_loop(0, chunks, chunk, 0)
    for c in range(chunks):
        results(c, False)


SMEM = pl.BlockSpec(memory_space=pltpu.SMEM)
VMEM = pl.BlockSpec(memory_space=pltpu.VMEM)
HBM = pl.BlockSpec(memory_space=pltpu.HBM)
DMA = pltpu.SemaphoreType.DMA


def in_hbm(x):
    return pltpu.with_memory_space_constraint(x, pltpu.HBM)


def call(kernel, name, out_shape, in_specs, out_specs, scratch=(), cost=(0, 0), aliases=None):
    return pl.pallas_call(
        kernel,
        out_shape=out_shape,
        in_specs=in_specs,
        out_specs=out_specs,
        scratch_shapes=list(scratch),
        compiler_params=pltpu.CompilerParams(vmem_limit_bytes=VMEM_BYTES),
        cost_estimate=pl.CostEstimate(flops=cost[0], bytes_accessed=cost[1], transcendentals=0),
        input_output_aliases=aliases or {},
        name=name,
    )


def swap(block, partner):
    n, lanes = lax.axis_size("ctx"), lax.axis_size("chan")
    route = []
    for i in range(n):
        for c in range(lanes):
            j = partner(i)
            to = j * lanes + c if j is not None else i * lanes + (c ^ 1)
            route.append((i * lanes + c, to))
    return lax.ppermute(block, ("ctx", "chan"), route)


def rotate(block, distance):
    n = lax.axis_size("ctx")
    return lax.ppermute(block, "ctx", [(i, (i + distance) % n) for i in range(n)])


def shards(q_feat, k_feat, v_feat, pole_rate, residue, skip_gain, lengths, owners):
    tok_dev, channels = q_feat.shape
    pole_count = pole_rate.shape[0]
    request_count = lengths.shape[0]
    n = lax.axis_size("ctx")
    width, halves = half_span(channels)
    chunks = tok_dev // CHUNK
    longest = n * tok_dev // 2
    hops = -(-(longest - 1) // tok_dev)
    element = tok_dev * channels * pole_count
    token_bytes = tok_dev * channels
    one = jax.ShapeDtypeStruct((pole_count, channels), F32)
    all_rows = jax.ShapeDtypeStruct((halves, tok_dev * SUBS, LANES), F32)
    state_shape = jax.ShapeDtypeStruct((pole_count * halves * SUBS, LANES), F32)
    saved_shape = jax.ShapeDtypeStruct(
        (halves, tok_dev // BLOCK * pole_count * SUBS, LANES), F32
    )
    tokens = pltpu.VMEM((tok_dev, channels), jnp.bfloat16)

    def blocks(count):
        return jax.ShapeDtypeStruct((count, pole_count, channels), F32)

    cross, pair_out, mine, u_rows, decays, gains, saved = call(
        pieces_kernel,
        "pieces",
        [one, blocks(1 + n // 2), blocks(n // 2), all_rows, state_shape, state_shape, saved_shape],
        [HBM] * 6,
        [VMEM] * 7,
        [
            tokens,
            tokens,
            pltpu.VMEM((pole_count, channels), F32),
            pltpu.VMEM((pole_count, channels), F32),
            pltpu.SMEM((request_count,), jnp.int32),
            pltpu.SMEM((request_count,), jnp.int32),
            pltpu.VMEM((request_count * pole_count * halves * SUBS, LANES), F32),
            DMA((2, chunks)),
            DMA((4,)),
        ],
        (2 * element, 8 * token_bytes),
    )(*map(in_hbm, (lengths, owners, k_feat, v_feat, pole_rate, residue)))

    def odd_partner(i):
        j = i + 1 if i % 2 else i - 1
        return j if 0 <= j < n else None

    odd_in = swap(cross, odd_partner)
    pair_in = swap(pair_out, lambda i: i ^ 1)
    skip_in = [rotate(cross, hop) for hop in range(2, hops + 1)]

    skip_rows = skip_gain.reshape(-1, LANES)
    if skip_rows.shape[0] < SUBS:
        skip_rows = jnp.pad(skip_rows, ((0, SUBS - skip_rows.shape[0]), (0, 0)))
    y_rows = call(
        taps_kernel,
        "taps",
        all_rows,
        [SMEM] + [VMEM] * 4,
        VMEM,
        [pltpu.VMEM((BLOCK * SUBS, LANES), F32)],
        (BLOCK * token_bytes, 8 * token_bytes),
    )(lengths, u_rows, decays, gains, skip_rows)

    pair_in, y_rows = lax.optimization_barrier((pair_in, y_rows))
    pooled = call(
        pool_kernel,
        "pool",
        [one] * (n // 2),
        [VMEM, VMEM],
        [VMEM] * (n // 2),
    )(mine, pair_in)
    decode_state = pooled[0]
    far_in = [rotate(block, 2 * d) for d, block in enumerate(pooled[1:], 1)]

    mixed_out = call(
        functools.partial(finish_kernel, hops - 1),
        "finish",
        jax.ShapeDtypeStruct((tok_dev, channels), jnp.bfloat16),
        [SMEM, VMEM, VMEM, HBM] + [VMEM] * (5 + hops - 1),
        HBM,
        [
            tokens,
            tokens,
            pltpu.VMEM((halves, CHUNK * SUBS, LANES), F32),
            pltpu.VMEM(state_shape.shape, F32),
            pltpu.VMEM((halves, pole_count * SUBS, LANES), F32),
            DMA((chunks,)),
            DMA((chunks,)),
        ],
        (2 * element, 8 * token_bytes),
    )(lengths, y_rows, saved, q_feat, decays, gains, pole_rate, pair_in, odd_in, *skip_in)
    return mixed_out, sum(far_in, decode_state)[None]


def solution(mesh):
    placed = (
        P(("groups", "ctx"), "chan"),
        P(("groups", "ctx"), "chan"),
        P(("groups", "ctx"), "chan"),
        P(None, "chan"),
        P(None, "chan"),
        P("chan"),
        P("groups"),
        P("groups"),
    )
    return jax.shard_map(
        shards,
        mesh=mesh,
        in_specs=placed,
        out_specs=(P(("groups", "ctx"), "chan"), P(("groups", "ctx"), None, "chan")),
        check_vma=False,
    )
```

```python
import functools

import jax
import jax.numpy as jnp
from jax import lax
from jax.experimental import pallas as pl
from jax.experimental.pallas import tpu as pltpu
from jax.sharding import PartitionSpec as P

LANES = 128
SUBS = 8
PACKED = 16
LOAD = 256
CHUNK = 128
BLOCK = 16
UNROLL = 8
VMEM_BYTES = 28 * 1024 * 1024
F32 = jnp.float32


def request_span(lengths_ref, request, request_count):
    start = jnp.int32(0)
    length = jnp.int32(0)
    for r in range(request_count):
        start = start + jnp.where(r < request, lengths_ref[r], 0)
        length = length + jnp.where(r == request, lengths_ref[r], 0)
    return start, start + length - 1


def request_at(lengths_ref, position, request_count):
    index = jnp.int32(-1)
    start = jnp.int32(0)
    for r in range(request_count):
        index = index + (start <= position).astype(jnp.int32)
        start = start + lengths_ref[r]
    return index


def request_before(lengths_ref, tok_dev, hop):
    first = lax.axis_index("ctx") * tok_dev
    return request_at(lengths_ref, first - (hop - 1) * tok_dev - 1, lengths_ref.shape[0])


def token_loop(lo, hi, step, carry):
    count = jnp.maximum(hi - lo, 0)
    groups = lax.shift_right_logical(count, jnp.int32(UNROLL.bit_length() - 1))

    def many(g, carry):
        base = lo + g * UNROLL
        for s in range(UNROLL):
            carry = step(base + s, carry)
        return carry

    carry = lax.fori_loop(0, groups, many, carry)
    return lax.fori_loop(lo + groups * UNROLL, lo + count, step, carry)


def half_span(channels):
    tiles = channels // LANES
    return min(tiles, SUBS), max(tiles // SUBS, 1)


def state_rows(p, h, halves):
    return pl.ds(pl.multiple_of((p * halves + h) * SUBS, SUBS), SUBS)


def natural_rows(p, tile, halves):
    return pl.ds((p * halves + tile // SUBS) * SUBS + tile % SUBS, SUBS, stride=halves * SUBS)


def token_rows(t):
    return pl.ds(
        lax.shift_right_logical(t, jnp.int32(3)) * (SUBS * SUBS) + lax.bitwise_and(t, jnp.int32(7)),
        SUBS,
        stride=SUBS,
    )


def block_token(b, s):
    return pl.ds(b * (BLOCK * SUBS) + s // SUBS * (SUBS * SUBS) + s % SUBS, SUBS, stride=SUBS)


def saved_rows(b, p, pole_count):
    return pl.ds(pl.multiple_of((b * pole_count + p) * SUBS, SUBS), SUBS)


def block_parts(lo, hi):
    head = jnp.minimum(hi, lax.bitwise_and(lo + (BLOCK - 1), jnp.int32(-BLOCK)))
    shift = jnp.int32(BLOCK.bit_length() - 1)
    first = lax.shift_right_logical(head + (BLOCK - 1), shift)
    last = jnp.maximum(lax.shift_right_logical(hi, shift), first)
    return head, first, last, jnp.maximum(last * BLOCK, head)


def tile_rows(group, j):
    return pl.ds(pl.multiple_of((group * SUBS + j) * SUBS, SUBS), SUBS)


def each_tile(value_ref):
    pole_count, channels = value_ref.shape
    for p in range(0, pole_count, SUBS):
        for tile in range(channels // LANES):
            yield p, tile, (slice(p, p + SUBS), slice(tile * LANES, (tile + 1) * LANES))


def to_states(ref, states, change):
    _, halves = half_span(ref.shape[1])
    for p, tile, at in each_tile(ref):
        states[natural_rows(p, tile, halves), :] = change(at)


def scaled(rate_ref, residue_ref, at):
    return residue_ref[at] * jnp.sqrt(1.0 - jnp.exp(-2.0 * rate_ref[at]))


def chunk_copy(src, src_at, dst, dst_at, sem, start):
    copy = pltpu.make_async_copy(src.at[src_at], dst.at[dst_at], sem)
    if start:
        copy.start()
    else:
        copy.wait()


def token_chunk(c, size=CHUNK):
    return pl.ds(pl.multiple_of(c * size, size), size)


def fill_rows(k_buf, v_buf, u_rows, c, first_tile, width):
    def block(b, _):
        rows = pl.ds(pl.multiple_of(c * LOAD + b * PACKED, PACKED), PACKED)
        for j in range(width):
            lanes = slice((first_tile + j) * LANES, (first_tile + j + 1) * LANES)
            u = k_buf[rows, lanes].astype(F32) * v_buf[rows, lanes].astype(F32)
            for part in range(PACKED // SUBS):
                group = c * (LOAD // SUBS) + b * (PACKED // SUBS) + part
                u_rows[tile_rows(group, j), :] = u[part * SUBS : (part + 1) * SUBS]
        return 0

    lax.fori_loop(0, LOAD // PACKED, block, 0)


def each_request(lengths_ref, base, extent, body):
    def request(r, start):
        length = lengths_ref[r]
        lo = jnp.maximum(start - base, 0)
        hi = jnp.minimum(start + length - base, extent)

        @pl.when(hi > lo)
        def _():
            body(r, start, lo, hi)

        return start + length

    lax.fori_loop(0, lengths_ref.shape[0], request, jnp.int32(0))


def total(terms):
    while len(terms) > 1:
        terms = [x + y for x, y in zip(terms[::2], terms[1::2])] + terms[len(terms) // 2 * 2 :]
    return terms[0]


def pieces_kernel(
    lengths_hbm, owners_hbm, k_hbm, v_hbm, rate_hbm, residue_hbm,
    cross_ref, near_ref, pair_ref, own_ref, mine_ref, u_rows, decays, gains, saved,
    k_buf, v_buf, rate_ref, residue_ref, lengths_ref, owners_ref, states, sems, small_sems,
):
    n = lax.axis_size("ctx")
    i = lax.axis_index("ctx")
    request_count = lengths_ref.shape[0]
    pole_count, channels = rate_ref.shape
    tok_dev = k_buf.shape[0]
    width, halves = half_span(channels)
    chunks = tok_dev // LOAD
    first = i * tok_dev
    last = first + tok_dev - 1

    def moves(c, start):
        rows = (token_chunk(c, LOAD), slice(None))
        chunk_copy(k_hbm, rows, k_buf, rows, sems.at[0, c], start)
        chunk_copy(v_hbm, rows, v_buf, rows, sems.at[1, c], start)

    small = [
        pltpu.make_async_copy(src, dst, small_sems.at[n])
        for n, (src, dst) in enumerate(
            (
                (lengths_hbm, lengths_ref),
                (owners_hbm, owners_ref),
                (rate_hbm, rate_ref),
                (residue_hbm, residue_ref),
            )
        )
    ]
    for copy in small:
        copy.start()
    for c in range(chunks):
        moves(c, True)

    def clear(b, _):
        states[pl.ds(pl.multiple_of(b * SUBS, SUBS), SUBS), :] = jnp.zeros((SUBS, LANES), F32)
        return 0

    lax.fori_loop(0, request_count * pole_count * halves, clear, 0)
    for copy in small:
        copy.wait()
    to_states(rate_ref, decays, lambda at: jnp.exp(-rate_ref[at]))
    to_states(rate_ref, gains, lambda at: scaled(rate_ref, residue_ref, at))

    def chunk(c, _):
        moves(c, False)
        for h in range(halves):
            fill_rows(k_buf, v_buf, u_rows.at[h], c, h * SUBS, width)
        base = c * LOAD

        def request(r, start, lo, hi):
            head, begin, end, tail = block_parts(base + lo, base + hi)

            def half(h, _):
                decay = [decays[state_rows(p, h, halves), :] for p in range(pole_count)]
                row = r * pole_count
                state = tuple(
                    states[state_rows(row + p, h, halves), :] for p in range(pole_count)
                )

                def advance(state, u):
                    return tuple(s * a + u for s, a in zip(state, decay))

                def single(t, state):
                    return advance(state, u_rows[h, token_rows(t), :])

                def save(b, state):
                    for p in range(pole_count):
                        saved[h, saved_rows(b, p, pole_count), :] = state[p]

                def block(b, state):
                    save(b, state)
                    for s in range(BLOCK):
                        state = advance(state, u_rows[h, block_token(b, s), :])
                    return state

                state = lax.fori_loop(base + lo, head, single, state)
                state = lax.fori_loop(begin, end, block, state)

                @pl.when(base + hi > tail)
                def _():
                    save(end, state)

                state = lax.fori_loop(tail, base + hi, single, state)
                for p in range(pole_count):
                    states[state_rows(row + p, h, halves), :] = state[p]
                return 0

            lax.fori_loop(0, halves, half, 0)

        each_request(lengths_ref, first + base, LOAD, request)
        return 0

    lax.fori_loop(0, chunks, chunk, 0)

    def owned(slot):
        request = jnp.int32(0)
        found = jnp.int32(0)
        for r in range(request_count):
            match = (owners_ref[r] == slot).astype(jnp.int32)
            request = request + r * match
            found = found + match
        start, end = request_span(lengths_ref, request, request_count)
        live = (found > 0) & (start <= last) & (end >= first)
        return request, jnp.maximum(end - last, 0), live

    def emit(out_ref, what):
        request, steps, live = what
        back = -steps.astype(F32)
        keep = jnp.where(live, 1.0, 0.0).astype(F32)
        for p, tile, at in each_tile(rate_ref):
            state = states[natural_rows(request * pole_count + p, tile, halves), :]
            out_ref[at] = state * (jnp.exp(rate_ref[at] * back) * keep)

    partner = jnp.where(lax.rem(i, 2) == 1, i - 1, i + 1)
    crossing = request_at(lengths_ref, last, request_count)
    for p, tile, at in each_tile(rate_ref):
        cross_ref[at] = states[natural_rows(crossing * pole_count + p, tile, halves), :]
    emit(near_ref, owned(partner))
    emit(own_ref, owned(i))
    for d in range(1, n // 2):
        emit(pair_ref.at[d - 1], owned(lax.rem(partner + 2 * d, n)))
        emit(mine_ref.at[d - 1], owned(lax.rem(i + 2 * d, n)))


def taps_kernel(lengths_ref, u_rows, decays, gains, skip_ref, y_rows, taps):
    halves = u_rows.shape[0]
    tok_dev = u_rows.shape[1] // SUBS
    pole_count = decays.shape[0] // (halves * SUBS)
    first = lax.axis_index("ctx") * tok_dev

    def half(h, _):
        skip = skip_ref[pl.ds(pl.multiple_of(h * SUBS, SUBS), SUBS), :]
        decay = [decays[state_rows(p, h, halves), :] for p in range(pole_count)]
        power = [gains[state_rows(p, h, halves), :] for p in range(pole_count)]
        for j in range(BLOCK):
            tap = total(list(power))
            taps[j * SUBS : (j + 1) * SUBS, :] = tap + skip if j == 0 else tap
            power = [x * a for x, a in zip(power, decay)]

        def request(r, start, lo, hi):
            head, begin, end, tail = block_parts(lo, hi)

            def alone(lo, hi):
                decay = [decays[state_rows(p, h, halves), :] for p in range(pole_count)]
                gain = [gains[state_rows(p, h, halves), :] for p in range(pole_count)]

                def single(t, state):
                    u = u_rows[h, token_rows(t), :]
                    state = tuple(s * a + u for s, a in zip(state, decay))
                    y_rows[h, token_rows(t), :] = total(
                        [s * g for s, g in zip(state, gain)] + [skip * u]
                    )
                    return state

                zero = jnp.zeros((SUBS, LANES), F32)
                lax.fori_loop(lo, hi, single, (zero,) * pole_count)

            @pl.when(head > lo)
            def _():
                alone(lo, head)

            @pl.when(hi > tail)
            def _():
                alone(tail, hi)

            tap = [taps[j * SUBS : (j + 1) * SUBS, :] for j in range(BLOCK)]

            def block(b, _):
                u = [u_rows[h, block_token(b, s), :] for s in range(BLOCK)]
                for s in range(BLOCK):
                    y_rows[h, block_token(b, s), :] = total(
                        [tap[j] * u[s - j] for j in range(s + 1)]
                    )
                return 0

            lax.fori_loop(begin, end, block, 0)

        each_request(lengths_ref, first, tok_dev, request)
        return 0

    lax.fori_loop(0, halves, half, 0)


def pool_kernel(mine_ref, pair_ref, *pooled_refs):
    for d, ref in enumerate(pooled_refs):
        for _, _, at in each_tile(ref):
            ref[at] = mine_ref[d, at[0], at[1]] + pair_ref[d, at[0], at[1]]


def finish_kernel(late, hops, lengths_ref, y_rows, saved, q_ref, decays, gains, rate_ref, *rest):
    hop_refs = rest[:hops]
    out_hbm, out_buf, w_rows, spread, fading, out_sems = rest[hops + int(late) :]
    tok_dev, channels = q_ref.shape
    halves = y_rows.shape[0]
    pole_count = rate_ref.shape[0]
    width, _ = half_span(channels)
    chunks = tok_dev // CHUNK
    first = lax.axis_index("ctx") * tok_dev
    before = request_before(lengths_ref, tok_dev, 1)
    reached = [
        (before >= 0) & (request_before(lengths_ref, tok_dev, hop) == before)
        for hop in range(1, max(hops, 2) + 1)
    ]
    _, end = request_span(lengths_ref, before, lengths_ref.shape[0])
    split = jnp.where(reached[1], jnp.minimum(end + 1 - first, tok_dev), 0)
    split = lax.div(split + (CHUNK - 1), jnp.int32(CHUNK))
    from_chunk, to_chunk = (0, split) if late else (split, chunks)

    def results(c, start):
        rows = (token_chunk(c), slice(None))
        chunk_copy(out_buf, rows, out_hbm, rows, out_sems.at[c], start)

    def incoming(at):
        state = jnp.zeros((SUBS, LANES), F32)
        for hop, ref in enumerate(hop_refs):
            moved = ref[at] * jnp.exp(rate_ref[at] * -float(hop * tok_dev)) if hop else ref[at]
            state = state + jnp.where(reached[hop], moved, 0.0)
        return state

    @pl.when(from_chunk < to_chunk)
    def _():
        to_states(rate_ref, spread, incoming)
        for p in range(pole_count):
            for h in range(halves):
                at = state_rows(p, h, halves)
                fading[h, state_rows(p, 0, 1), :] = spread[at, :] * gains[at, :] * decays[at, :]

    def gate(c):
        def block(b, _):
            rows = pl.ds(pl.multiple_of(c * CHUNK + b * PACKED, PACKED), PACKED)
            for h in range(halves):
                for j in range(width):
                    lanes = slice((h * SUBS + j) * LANES, (h * SUBS + j + 1) * LANES)
                    w = jnp.concatenate(
                        [
                            w_rows[h, tile_rows(b * (PACKED // SUBS) + part, j), :]
                            for part in range(PACKED // SUBS)
                        ],
                        axis=0,
                    )
                    out_buf[rows, lanes] = (q_ref[rows, lanes].astype(F32) * w).astype(jnp.bfloat16)
            return 0

        lax.fori_loop(0, CHUNK // PACKED, block, 0)

    def chunk(c, _):
        base = c * CHUNK

        def request(r, start, lo, hi):
            head, begin, end, tail = block_parts(lo, hi)

            def half(h, _):
                y = y_rows.at[h, pl.ds(pl.multiple_of(base * SUBS, CHUNK * SUBS), CHUNK * SUBS)]
                w = w_rows.at[h]

                @pl.when(start >= first)
                def _():
                    fading[h] = jnp.zeros(fading.shape[1:], F32)

                def keep(t, _):
                    w[token_rows(t), :] = y[token_rows(t), :]
                    return 0

                lax.fori_loop(lo, head, keep, 0)
                decay = [decays[state_rows(p, h, halves), :] for p in range(pole_count)]

                def opening(b):
                    state = []
                    for p in range(pole_count):
                        at = state_rows(p, h, halves)
                        local = saved[h, saved_rows(base // BLOCK + b, p, pole_count), :]
                        state.append(
                            local * (gains[at, :] * decays[at, :])
                            + fading[h, state_rows(p, 0, 1), :]
                        )
                    return state

                def block(b, _):
                    state = opening(b)
                    for p in range(pole_count):
                        at = state_rows(p, 0, 1)
                        power = decay[p]
                        for _ in range(BLOCK.bit_length() - 1):
                            power = power * power
                        fading[h, at, :] = fading[h, at, :] * power
                    for s in range(BLOCK):
                        rows = block_token(b, s)
                        w[rows, :] = y[rows, :] + total(list(state))
                        if s < BLOCK - 1:
                            state = [x * a for x, a in zip(state, decay)]
                    return 0

                lax.fori_loop(begin, end, block, 0)

                @pl.when(hi > tail)
                def _():
                    def single(t, state):
                        w[token_rows(t), :] = y[token_rows(t), :] + total(list(state))
                        return tuple(x * a for x, a in zip(state, decay))

                    lax.fori_loop(tail, hi, single, tuple(opening(end)))

                return 0

            lax.fori_loop(0, halves, half, 0)

        each_request(lengths_ref, first + base, CHUNK, request)
        gate(c)
        results(c, True)
        return 0

    def drain(c, _):
        results(c, False)
        return 0

    lax.fori_loop(from_chunk, to_chunk, chunk, 0)
    lax.fori_loop(from_chunk, to_chunk, drain, 0)


SMEM = pl.BlockSpec(memory_space=pltpu.SMEM)
VMEM = pl.BlockSpec(memory_space=pltpu.VMEM)
HBM = pl.BlockSpec(memory_space=pltpu.HBM)
DMA = pltpu.SemaphoreType.DMA


def in_hbm(x):
    return pltpu.with_memory_space_constraint(x, pltpu.HBM)


def call(kernel, name, out_shape, in_specs, out_specs, scratch=(), cost=(0, 0), aliases=None):
    return pl.pallas_call(
        kernel,
        out_shape=out_shape,
        in_specs=in_specs,
        out_specs=out_specs,
        scratch_shapes=list(scratch),
        compiler_params=pltpu.CompilerParams(vmem_limit_bytes=VMEM_BYTES),
        cost_estimate=pl.CostEstimate(flops=cost[0], bytes_accessed=cost[1], transcendentals=0),
        input_output_aliases=aliases or {},
        name=name,
    )


def rotate(block, distance):
    n = lax.axis_size("ctx")
    return lax.ppermute(block, "ctx", [(i, (i + distance) % n) for i in range(n)])


def trade(block):
    n = lax.axis_size("ctx")
    return lax.ppermute(block, "ctx", [(i, i ^ 1) for i in range(n)])


def shards(q_feat, k_feat, v_feat, pole_rate, residue, skip_gain, lengths, owners):
    tok_dev, channels = q_feat.shape
    pole_count = pole_rate.shape[0]
    request_count = lengths.shape[0]
    n = lax.axis_size("ctx")
    width, halves = half_span(channels)
    chunks = tok_dev // CHUNK
    longest = n * tok_dev // 2
    hops = -(-(longest - 1) // tok_dev)
    element = tok_dev * channels * pole_count
    token_bytes = tok_dev * channels
    one = jax.ShapeDtypeStruct((pole_count, channels), F32)
    all_rows = jax.ShapeDtypeStruct((halves, tok_dev * SUBS, LANES), F32)
    state_shape = jax.ShapeDtypeStruct((pole_count * halves * SUBS, LANES), F32)
    saved_shape = jax.ShapeDtypeStruct(
        (halves, tok_dev // BLOCK * pole_count * SUBS, LANES), F32
    )
    tokens = pltpu.VMEM((tok_dev, channels), jnp.bfloat16)

    def blocks(count):
        return jax.ShapeDtypeStruct((count, pole_count, channels), F32)

    cross, near_out, pair_out, own, mine, u_rows, decays, gains, saved = call(
        pieces_kernel,
        "pieces",
        [one, one, blocks(n // 2 - 1), one, blocks(n // 2 - 1)]
        + [all_rows, state_shape, state_shape, saved_shape],
        [HBM] * 6,
        [VMEM] * 9,
        [
            tokens,
            tokens,
            pltpu.VMEM((pole_count, channels), F32),
            pltpu.VMEM((pole_count, channels), F32),
            pltpu.SMEM((request_count,), jnp.int32),
            pltpu.SMEM((request_count,), jnp.int32),
            pltpu.VMEM((request_count * pole_count * halves * SUBS, LANES), F32),
            DMA((2, tok_dev // LOAD)),
            DMA((4,)),
        ],
        (2 * element, 8 * token_bytes),
    )(*map(in_hbm, (lengths, owners, k_feat, v_feat, pole_rate, residue)))

    hop_in = [rotate(cross, 1)]
    pair_in = trade(pair_out)
    hop_in += [rotate(cross, hop) for hop in range(2, hops + 1)]

    skip_rows = skip_gain.reshape(-1, LANES)
    if skip_rows.shape[0] < SUBS:
        skip_rows = jnp.pad(skip_rows, ((0, SUBS - skip_rows.shape[0]), (0, 0)))
    y_rows = call(
        taps_kernel,
        "taps",
        all_rows,
        [SMEM] + [VMEM] * 4,
        VMEM,
        [pltpu.VMEM((BLOCK * SUBS, LANES), F32)],
        (BLOCK * token_bytes, 8 * token_bytes),
    )(lengths, u_rows, decays, gains, skip_rows)

    pair_in, near_out, y_rows = lax.optimization_barrier((pair_in, near_out, y_rows))
    far_out = call(
        pool_kernel, "pool", [one] * (n // 2 - 1), [VMEM] * 2, [VMEM] * (n // 2 - 1)
    )(mine, pair_in)
    far_in = [rotate(block, 2 * d) for d, block in enumerate(far_out, 1)]
    near_in = trade(near_out)

    mixed_shape = jax.ShapeDtypeStruct((tok_dev, channels), jnp.bfloat16)

    def finish(late, used, more):
        operands = [lengths, y_rows, saved, q_feat, decays, gains, pole_rate, *used]
        return call(
            functools.partial(finish_kernel, late, len(used)),
            "late" if late else "finish",
            mixed_shape,
            [SMEM] + [VMEM] * (6 + len(used)) + [HBM] * len(more),
            HBM,
            [
                tokens,
                pltpu.VMEM((halves, CHUNK * SUBS, LANES), F32),
                pltpu.VMEM(state_shape.shape, F32),
                pltpu.VMEM((halves, pole_count * SUBS, LANES), F32),
                DMA((chunks,)),
            ],
            (2 * element, 8 * token_bytes),
            {len(operands): 0} if late else None,
        )(*operands, *more)

    mixed_out = finish(True, hop_in, [finish(False, hop_in[:1], [])])
    return mixed_out, sum(far_in, own + near_in)[None]


def solution(mesh):
    placed = (
        P(("groups", "ctx"), "chan"),
        P(("groups", "ctx"), "chan"),
        P(("groups", "ctx"), "chan"),
        P(None, "chan"),
        P(None, "chan"),
        P("chan"),
        P("groups"),
        P("groups"),
    )
    return jax.shard_map(
        shards,
        mesh=mesh,
        in_specs=placed,
        out_specs=(P(("groups", "ctx"), "chan"), P(("groups", "ctx"), None, "chan")),
        check_vma=False,
    )
```

```python
import functools

import jax
import jax.numpy as jnp
from jax import lax
from jax.experimental import pallas as pl
from jax.experimental.pallas import tpu as pltpu
from jax.sharding import PartitionSpec as P

LANES = 128
SUBS = 8
PACKED = 16
LOAD = 256
CHUNK = 128
BLOCK = 16
UNROLL = 8
VMEM_BYTES = 28 * 1024 * 1024
F32 = jnp.float32


def request_span(lengths_ref, request, request_count):
    start = jnp.int32(0)
    length = jnp.int32(0)
    for r in range(request_count):
        start = start + jnp.where(r < request, lengths_ref[r], 0)
        length = length + jnp.where(r == request, lengths_ref[r], 0)
    return start, start + length - 1


def request_at(lengths_ref, position, request_count):
    index = jnp.int32(-1)
    start = jnp.int32(0)
    for r in range(request_count):
        index = index + (start <= position).astype(jnp.int32)
        start = start + lengths_ref[r]
    return index


def request_before(lengths_ref, tok_dev, hop):
    first = lax.axis_index("ctx") * tok_dev
    return request_at(lengths_ref, first - (hop - 1) * tok_dev - 1, lengths_ref.shape[0])


def token_loop(lo, hi, step, carry):
    count = jnp.maximum(hi - lo, 0)
    groups = lax.shift_right_logical(count, jnp.int32(UNROLL.bit_length() - 1))

    def many(g, carry):
        base = lo + g * UNROLL
        for s in range(UNROLL):
            carry = step(base + s, carry)
        return carry

    carry = lax.fori_loop(0, groups, many, carry)
    return lax.fori_loop(lo + groups * UNROLL, lo + count, step, carry)


def half_span(channels):
    tiles = channels // LANES
    return min(tiles, SUBS), max(tiles // SUBS, 1)


def state_rows(p, h, halves):
    return pl.ds(pl.multiple_of((p * halves + h) * SUBS, SUBS), SUBS)


def natural_rows(p, tile, halves):
    return pl.ds((p * halves + tile // SUBS) * SUBS + tile % SUBS, SUBS, stride=halves * SUBS)


def token_rows(t):
    return pl.ds(
        lax.shift_right_logical(t, jnp.int32(3)) * (SUBS * SUBS) + lax.bitwise_and(t, jnp.int32(7)),
        SUBS,
        stride=SUBS,
    )


def block_token(b, s):
    return pl.ds(b * (BLOCK * SUBS) + s // SUBS * (SUBS * SUBS) + s % SUBS, SUBS, stride=SUBS)


def saved_rows(b, p, pole_count):
    return pl.ds(pl.multiple_of((b * pole_count + p) * SUBS, SUBS), SUBS)


def block_parts(lo, hi):
    head = jnp.minimum(hi, lax.bitwise_and(lo + (BLOCK - 1), jnp.int32(-BLOCK)))
    shift = jnp.int32(BLOCK.bit_length() - 1)
    first = lax.shift_right_logical(head + (BLOCK - 1), shift)
    last = jnp.maximum(lax.shift_right_logical(hi, shift), first)
    return head, first, last, jnp.maximum(last * BLOCK, head)


def tile_rows(group, j):
    return pl.ds(pl.multiple_of((group * SUBS + j) * SUBS, SUBS), SUBS)


def each_tile(value_ref):
    pole_count, channels = value_ref.shape
    for p in range(0, pole_count, SUBS):
        for tile in range(channels // LANES):
            yield p, tile, (slice(p, p + SUBS), slice(tile * LANES, (tile + 1) * LANES))


def to_states(ref, states, change):
    _, halves = half_span(ref.shape[1])
    for p, tile, at in each_tile(ref):
        states[natural_rows(p, tile, halves), :] = change(at)


def scaled(rate_ref, residue_ref, at):
    return residue_ref[at] * jnp.sqrt(1.0 - jnp.exp(-2.0 * rate_ref[at]))


def chunk_copy(src, src_at, dst, dst_at, sem, start):
    copy = pltpu.make_async_copy(src.at[src_at], dst.at[dst_at], sem)
    if start:
        copy.start()
    else:
        copy.wait()


def token_chunk(c, size=CHUNK):
    return pl.ds(pl.multiple_of(c * size, size), size)


def fill_rows(k_buf, v_buf, u_rows, c, first_tile, width):
    def block(b, _):
        rows = pl.ds(pl.multiple_of(c * LOAD + b * PACKED, PACKED), PACKED)
        for j in range(width):
            lanes = slice((first_tile + j) * LANES, (first_tile + j + 1) * LANES)
            u = k_buf[rows, lanes].astype(F32) * v_buf[rows, lanes].astype(F32)
            for part in range(PACKED // SUBS):
                group = c * (LOAD // SUBS) + b * (PACKED // SUBS) + part
                u_rows[tile_rows(group, j), :] = u[part * SUBS : (part + 1) * SUBS]
        return 0

    lax.fori_loop(0, LOAD // PACKED, block, 0)


def fill_lengths(bounds_ref, lengths_ref):
    for r in range(bounds_ref.shape[0]):
        lengths_ref[r] = jnp.max(bounds_ref[r]).astype(jnp.int32)


def each_request(lengths_ref, base, extent, body):
    def request(r, start):
        length = lengths_ref[r]
        lo = jnp.maximum(start - base, 0)
        hi = jnp.minimum(start + length - base, extent)

        @pl.when(hi > lo)
        def _():
            body(r, start, lo, hi)

        return start + length

    lax.fori_loop(0, lengths_ref.shape[0], request, jnp.int32(0))


def total(terms):
    while len(terms) > 1:
        terms = [x + y for x, y in zip(terms[::2], terms[1::2])] + terms[len(terms) // 2 * 2 :]
    return terms[0]


def pieces_kernel(
    lengths_hbm, owners_hbm, k_hbm, v_hbm, rate_hbm, residue_hbm,
    cross_ref, near_ref, pair_ref, own_ref, mine_ref, bounds_ref, u_rows, decays, gains, saved,
    k_buf, v_buf, rate_ref, residue_ref, lengths_ref, owners_ref, states, sems, small_sems,
):
    n = lax.axis_size("ctx")
    i = lax.axis_index("ctx")
    request_count = lengths_ref.shape[0]
    pole_count, channels = rate_ref.shape
    tok_dev = k_buf.shape[0]
    width, halves = half_span(channels)
    chunks = tok_dev // LOAD
    first = i * tok_dev
    last = first + tok_dev - 1

    def moves(c, start):
        rows = (token_chunk(c, LOAD), slice(None))
        chunk_copy(k_hbm, rows, k_buf, rows, sems.at[0, c], start)
        chunk_copy(v_hbm, rows, v_buf, rows, sems.at[1, c], start)

    small = [
        pltpu.make_async_copy(src, dst, small_sems.at[n])
        for n, (src, dst) in enumerate(
            (
                (lengths_hbm, lengths_ref),
                (owners_hbm, owners_ref),
                (rate_hbm, rate_ref),
                (residue_hbm, residue_ref),
            )
        )
    ]
    for copy in small:
        copy.start()
    for c in range(chunks):
        moves(c, True)

    def clear(b, _):
        states[pl.ds(pl.multiple_of(b * SUBS, SUBS), SUBS), :] = jnp.zeros((SUBS, LANES), F32)
        return 0

    lax.fori_loop(0, request_count * pole_count * halves, clear, 0)
    for copy in small:
        copy.wait()
    for r in range(request_count):
        bounds_ref[r] = jnp.full((SUBS, LANES), lengths_ref[r].astype(F32), F32)
    to_states(rate_ref, decays, lambda at: jnp.exp(-rate_ref[at]))
    to_states(rate_ref, gains, lambda at: scaled(rate_ref, residue_ref, at))

    def chunk(c, _):
        moves(c, False)
        for h in range(halves):
            fill_rows(k_buf, v_buf, u_rows.at[h], c, h * SUBS, width)
        base = c * LOAD

        def request(r, start, lo, hi):
            head, begin, end, tail = block_parts(base + lo, base + hi)

            def half(h, _):
                decay = [decays[state_rows(p, h, halves), :] for p in range(pole_count)]
                row = r * pole_count
                state = tuple(
                    states[state_rows(row + p, h, halves), :] for p in range(pole_count)
                )

                def advance(state, u):
                    return tuple(s * a + u for s, a in zip(state, decay))

                def single(t, state):
                    return advance(state, u_rows[h, token_rows(t), :])

                def save(b, state):
                    for p in range(pole_count):
                        saved[h, saved_rows(b, p, pole_count), :] = state[p]

                def block(b, state):
                    save(b, state)
                    for s in range(BLOCK):
                        state = advance(state, u_rows[h, block_token(b, s), :])
                    return state

                state = lax.fori_loop(base + lo, head, single, state)
                state = lax.fori_loop(begin, end, block, state)

                @pl.when(base + hi > tail)
                def _():
                    save(end, state)

                state = lax.fori_loop(tail, base + hi, single, state)
                for p in range(pole_count):
                    states[state_rows(row + p, h, halves), :] = state[p]
                return 0

            lax.fori_loop(0, halves, half, 0)

        each_request(lengths_ref, first + base, LOAD, request)
        return 0

    lax.fori_loop(0, chunks, chunk, 0)

    def owned(slot):
        request = jnp.int32(0)
        found = jnp.int32(0)
        for r in range(request_count):
            match = (owners_ref[r] == slot).astype(jnp.int32)
            request = request + r * match
            found = found + match
        start, end = request_span(lengths_ref, request, request_count)
        live = (found > 0) & (start <= last) & (end >= first)
        return request, jnp.maximum(end - last, 0), live

    def emit(out_ref, what):
        request, steps, live = what
        back = -steps.astype(F32)
        keep = jnp.where(live, 1.0, 0.0).astype(F32)
        for p, tile, at in each_tile(rate_ref):
            state = states[natural_rows(request * pole_count + p, tile, halves), :]
            out_ref[at] = state * (jnp.exp(rate_ref[at] * back) * keep)

    partner = jnp.where(lax.rem(i, 2) == 1, i - 1, i + 1)
    crossing = request_at(lengths_ref, last, request_count)
    for p, tile, at in each_tile(rate_ref):
        cross_ref[at] = states[natural_rows(crossing * pole_count + p, tile, halves), :]
    emit(near_ref, owned(partner))
    emit(own_ref, owned(i))
    for d in range(1, n // 2):
        emit(pair_ref.at[d - 1], owned(lax.rem(partner + 2 * d, n)))
        emit(mine_ref.at[d - 1], owned(lax.rem(i + 2 * d, n)))


def taps_kernel(bounds_ref, u_rows, decays, gains, skip_ref, y_rows, taps, lengths_ref):
    fill_lengths(bounds_ref, lengths_ref)
    halves = u_rows.shape[0]
    tok_dev = u_rows.shape[1] // SUBS
    pole_count = decays.shape[0] // (halves * SUBS)
    first = lax.axis_index("ctx") * tok_dev

    def half(h, _):
        skip = skip_ref[pl.ds(pl.multiple_of(h * SUBS, SUBS), SUBS), :]
        decay = [decays[state_rows(p, h, halves), :] for p in range(pole_count)]
        power = [gains[state_rows(p, h, halves), :] for p in range(pole_count)]
        for j in range(BLOCK):
            tap = total(list(power))
            taps[j * SUBS : (j + 1) * SUBS, :] = tap + skip if j == 0 else tap
            power = [x * a for x, a in zip(power, decay)]

        def request(r, start, lo, hi):
            head, begin, end, tail = block_parts(lo, hi)

            def alone(lo, hi):
                decay = [decays[state_rows(p, h, halves), :] for p in range(pole_count)]
                gain = [gains[state_rows(p, h, halves), :] for p in range(pole_count)]

                def single(t, state):
                    u = u_rows[h, token_rows(t), :]
                    state = tuple(s * a + u for s, a in zip(state, decay))
                    y_rows[h, token_rows(t), :] = total(
                        [s * g for s, g in zip(state, gain)] + [skip * u]
                    )
                    return state

                zero = jnp.zeros((SUBS, LANES), F32)
                lax.fori_loop(lo, hi, single, (zero,) * pole_count)

            @pl.when(head > lo)
            def _():
                alone(lo, head)

            @pl.when(hi > tail)
            def _():
                alone(tail, hi)

            tap = [taps[j * SUBS : (j + 1) * SUBS, :] for j in range(BLOCK)]

            def block(b, _):
                u = [u_rows[h, block_token(b, s), :] for s in range(BLOCK)]
                for s in range(BLOCK):
                    y_rows[h, block_token(b, s), :] = total(
                        [tap[j] * u[s - j] for j in range(s + 1)]
                    )
                return 0

            lax.fori_loop(begin, end, block, 0)

        each_request(lengths_ref, first, tok_dev, request)
        return 0

    lax.fori_loop(0, halves, half, 0)


def pool_kernel(mine_ref, pair_ref, *pooled_refs):
    for d, ref in enumerate(pooled_refs):
        for _, _, at in each_tile(ref):
            ref[at] = mine_ref[d, at[0], at[1]] + pair_ref[d, at[0], at[1]]


def finish_kernel(late, hops, bounds_ref, y_rows, saved, q_ref, decays, gains, rate_ref, *rest):
    hop_refs = rest[:hops]
    out_hbm, out_buf, w_rows, spread, fading, lengths_ref, out_sems = rest[hops + int(late) :]
    fill_lengths(bounds_ref, lengths_ref)
    tok_dev, channels = q_ref.shape
    halves = y_rows.shape[0]
    pole_count = rate_ref.shape[0]
    width, _ = half_span(channels)
    chunks = tok_dev // CHUNK
    first = lax.axis_index("ctx") * tok_dev
    before = request_before(lengths_ref, tok_dev, 1)
    reached = [
        (before >= 0) & (request_before(lengths_ref, tok_dev, hop) == before)
        for hop in range(1, max(hops, 2) + 1)
    ]
    _, end = request_span(lengths_ref, before, lengths_ref.shape[0])
    split = jnp.where(reached[1], jnp.minimum(end + 1 - first, tok_dev), 0)
    split = lax.div(split + (CHUNK - 1), jnp.int32(CHUNK))
    from_chunk, to_chunk = (0, split) if late else (split, chunks)

    def results(c, start):
        rows = (token_chunk(c), slice(None))
        chunk_copy(out_buf, rows, out_hbm, rows, out_sems.at[c], start)

    def incoming(at):
        state = jnp.zeros((SUBS, LANES), F32)
        for hop, ref in enumerate(hop_refs):
            moved = ref[at] * jnp.exp(rate_ref[at] * -float(hop * tok_dev)) if hop else ref[at]
            state = state + jnp.where(reached[hop], moved, 0.0)
        return state

    @pl.when(from_chunk < to_chunk)
    def _():
        to_states(rate_ref, spread, incoming)
        for p in range(pole_count):
            for h in range(halves):
                at = state_rows(p, h, halves)
                fading[h, state_rows(p, 0, 1), :] = spread[at, :] * gains[at, :] * decays[at, :]

    def gate(c):
        def block(b, _):
            rows = pl.ds(pl.multiple_of(c * CHUNK + b * PACKED, PACKED), PACKED)
            for h in range(halves):
                for j in range(width):
                    lanes = slice((h * SUBS + j) * LANES, (h * SUBS + j + 1) * LANES)
                    w = jnp.concatenate(
                        [
                            w_rows[h, tile_rows(b * (PACKED // SUBS) + part, j), :]
                            for part in range(PACKED // SUBS)
                        ],
                        axis=0,
                    )
                    out_buf[rows, lanes] = (q_ref[rows, lanes].astype(F32) * w).astype(jnp.bfloat16)
            return 0

        lax.fori_loop(0, CHUNK // PACKED, block, 0)

    def chunk(c, _):
        base = c * CHUNK

        def request(r, start, lo, hi):
            head, begin, end, tail = block_parts(lo, hi)

            def half(h, _):
                y = y_rows.at[h, pl.ds(pl.multiple_of(base * SUBS, CHUNK * SUBS), CHUNK * SUBS)]
                w = w_rows.at[h]

                @pl.when(start >= first)
                def _():
                    fading[h] = jnp.zeros(fading.shape[1:], F32)

                def keep(t, _):
                    w[token_rows(t), :] = y[token_rows(t), :]
                    return 0

                lax.fori_loop(lo, head, keep, 0)
                decay = [decays[state_rows(p, h, halves), :] for p in range(pole_count)]

                def opening(b):
                    state = []
                    for p in range(pole_count):
                        at = state_rows(p, h, halves)
                        local = saved[h, saved_rows(base // BLOCK + b, p, pole_count), :]
                        state.append(
                            local * (gains[at, :] * decays[at, :])
                            + fading[h, state_rows(p, 0, 1), :]
                        )
                    return state

                def block(b, _):
                    state = opening(b)
                    for p in range(pole_count):
                        at = state_rows(p, 0, 1)
                        power = decay[p]
                        for _ in range(BLOCK.bit_length() - 1):
                            power = power * power
                        fading[h, at, :] = fading[h, at, :] * power
                    for s in range(BLOCK):
                        rows = block_token(b, s)
                        w[rows, :] = y[rows, :] + total(list(state))
                        if s < BLOCK - 1:
                            state = [x * a for x, a in zip(state, decay)]
                    return 0

                lax.fori_loop(begin, end, block, 0)

                @pl.when(hi > tail)
                def _():
                    def single(t, state):
                        w[token_rows(t), :] = y[token_rows(t), :] + total(list(state))
                        return tuple(x * a for x, a in zip(state, decay))

                    lax.fori_loop(tail, hi, single, tuple(opening(end)))

                return 0

            lax.fori_loop(0, halves, half, 0)

        each_request(lengths_ref, first + base, CHUNK, request)
        gate(c)
        results(c, True)
        return 0

    def drain(c, _):
        results(c, False)
        return 0

    lax.fori_loop(from_chunk, to_chunk, chunk, 0)
    lax.fori_loop(from_chunk, to_chunk, drain, 0)


SMEM = pl.BlockSpec(memory_space=pltpu.SMEM)
VMEM = pl.BlockSpec(memory_space=pltpu.VMEM)
HBM = pl.BlockSpec(memory_space=pltpu.HBM)
DMA = pltpu.SemaphoreType.DMA


def in_hbm(x):
    return pltpu.with_memory_space_constraint(x, pltpu.HBM)


def call(kernel, name, out_shape, in_specs, out_specs, scratch=(), cost=(0, 0), aliases=None):
    return pl.pallas_call(
        kernel,
        out_shape=out_shape,
        in_specs=in_specs,
        out_specs=out_specs,
        scratch_shapes=list(scratch),
        compiler_params=pltpu.CompilerParams(vmem_limit_bytes=VMEM_BYTES),
        cost_estimate=pl.CostEstimate(flops=cost[0], bytes_accessed=cost[1], transcendentals=0),
        input_output_aliases=aliases or {},
        name=name,
    )


def rotate(block, distance):
    n = lax.axis_size("ctx")
    return lax.ppermute(block, "ctx", [(i, (i + distance) % n) for i in range(n)])


def trade(block):
    n = lax.axis_size("ctx")
    return lax.ppermute(block, "ctx", [(i, i ^ 1) for i in range(n)])


def shards(q_feat, k_feat, v_feat, pole_rate, residue, skip_gain, lengths, owners):
    tok_dev, channels = q_feat.shape
    pole_count = pole_rate.shape[0]
    request_count = lengths.shape[0]
    n = lax.axis_size("ctx")
    width, halves = half_span(channels)
    chunks = tok_dev // CHUNK
    longest = n * tok_dev // 2
    hops = -(-(longest - 1) // tok_dev)
    element = tok_dev * channels * pole_count
    token_bytes = tok_dev * channels
    one = jax.ShapeDtypeStruct((pole_count, channels), F32)
    all_rows = jax.ShapeDtypeStruct((halves, tok_dev * SUBS, LANES), F32)
    state_shape = jax.ShapeDtypeStruct((pole_count * halves * SUBS, LANES), F32)
    saved_shape = jax.ShapeDtypeStruct(
        (halves, tok_dev // BLOCK * pole_count * SUBS, LANES), F32
    )
    tokens = pltpu.VMEM((tok_dev, channels), jnp.bfloat16)

    def blocks(count):
        return jax.ShapeDtypeStruct((count, pole_count, channels), F32)

    cross, near_out, pair_out, own, mine, bounds, u_rows, decays, gains, saved = call(
        pieces_kernel,
        "pieces",
        [one, one, blocks(n // 2 - 1), one, blocks(n // 2 - 1)]
        + [jax.ShapeDtypeStruct((request_count, SUBS, LANES), F32), all_rows, state_shape, state_shape, saved_shape],
        [HBM] * 6,
        [VMEM] * 10,
        [
            tokens,
            tokens,
            pltpu.VMEM((pole_count, channels), F32),
            pltpu.VMEM((pole_count, channels), F32),
            pltpu.SMEM((request_count,), jnp.int32),
            pltpu.SMEM((request_count,), jnp.int32),
            pltpu.VMEM((request_count * pole_count * halves * SUBS, LANES), F32),
            DMA((2, tok_dev // LOAD)),
            DMA((4,)),
        ],
        (2 * element, 8 * token_bytes),
    )(*map(in_hbm, (lengths, owners, k_feat, v_feat, pole_rate, residue)))

    hop_in = [rotate(cross, 1)]
    pair_in = trade(pair_out)
    hop_in += [rotate(cross, hop) for hop in range(2, hops + 1)]

    skip_rows = skip_gain.reshape(-1, LANES)
    if skip_rows.shape[0] < SUBS:
        skip_rows = jnp.pad(skip_rows, ((0, SUBS - skip_rows.shape[0]), (0, 0)))
    y_rows = call(
        taps_kernel,
        "taps",
        all_rows,
        [VMEM] * 5,
        VMEM,
        [pltpu.VMEM((BLOCK * SUBS, LANES), F32), pltpu.SMEM((request_count,), jnp.int32)],
        (BLOCK * token_bytes, 8 * token_bytes),
    )(bounds, u_rows, decays, gains, skip_rows)

    near_out, y_rows = lax.optimization_barrier((near_out, y_rows))
    near_in = trade(near_out)
    pair_in, y_rows = lax.optimization_barrier((pair_in, y_rows))
    far_out = call(
        pool_kernel, "pool", [one] * (n // 2 - 1), [VMEM] * 2, [VMEM] * (n // 2 - 1)
    )(mine, pair_in)
    far_in = [rotate(block, 2 * d) for d, block in enumerate(far_out, 1)]

    mixed_shape = jax.ShapeDtypeStruct((tok_dev, channels), jnp.bfloat16)

    def finish(late, used, more):
        operands = [bounds, y_rows, saved, q_feat, decays, gains, pole_rate, *used]
        return call(
            functools.partial(finish_kernel, late, len(used)),
            "late" if late else "finish",
            mixed_shape,
            [VMEM] * (7 + len(used)) + [HBM] * len(more),
            HBM,
            [
                tokens,
                pltpu.VMEM((halves, CHUNK * SUBS, LANES), F32),
                pltpu.VMEM(state_shape.shape, F32),
                pltpu.VMEM((halves, pole_count * SUBS, LANES), F32),
                pltpu.SMEM((request_count,), jnp.int32),
                DMA((chunks,)),
            ],
            (2 * element, 8 * token_bytes),
            {len(operands): 0} if late else None,
        )(*operands, *more)

    mixed_out = finish(True, hop_in, [finish(False, hop_in[:1], [])])
    return mixed_out, sum(far_in, own + near_in)[None]


def solution(mesh):
    placed = (
        P(("groups", "ctx"), "chan"),
        P(("groups", "ctx"), "chan"),
        P(("groups", "ctx"), "chan"),
        P(None, "chan"),
        P(None, "chan"),
        P("chan"),
        P("groups"),
        P("groups"),
    )
    return jax.shard_map(
        shards,
        mesh=mesh,
        in_specs=placed,
        out_specs=(P(("groups", "ctx"), "chan"), P(("groups", "ctx"), None, "chan")),
        check_vma=False,
    )
```

```python
import functools

import jax
import jax.numpy as jnp
from jax import lax
from jax.experimental import pallas as pl
from jax.experimental.pallas import tpu as pltpu
from jax.sharding import PartitionSpec as P

LANES = 128
SUBS = 8
PACKED = 16
LOAD = 256
CHUNK = 256
BLOCK = 16
UNROLL = 8
VMEM_BYTES = 28 * 1024 * 1024
F32 = jnp.float32


def request_span(lengths_ref, request, request_count):
    start = jnp.int32(0)
    length = jnp.int32(0)
    for r in range(request_count):
        start = start + jnp.where(r < request, lengths_ref[r], 0)
        length = length + jnp.where(r == request, lengths_ref[r], 0)
    return start, start + length - 1


def request_at(lengths_ref, position, request_count):
    index = jnp.int32(-1)
    start = jnp.int32(0)
    for r in range(request_count):
        index = index + (start <= position).astype(jnp.int32)
        start = start + lengths_ref[r]
    return index


def request_before(lengths_ref, tok_dev, hop):
    first = lax.axis_index("ctx") * tok_dev
    return request_at(lengths_ref, first - (hop - 1) * tok_dev - 1, lengths_ref.shape[0])


def token_loop(lo, hi, step, carry):
    count = jnp.maximum(hi - lo, 0)
    groups = lax.shift_right_logical(count, jnp.int32(UNROLL.bit_length() - 1))

    def many(g, carry):
        base = lo + g * UNROLL
        for s in range(UNROLL):
            carry = step(base + s, carry)
        return carry

    carry = lax.fori_loop(0, groups, many, carry)
    return lax.fori_loop(lo + groups * UNROLL, lo + count, step, carry)


def half_span(channels):
    tiles = channels // LANES
    return min(tiles, SUBS), max(tiles // SUBS, 1)


def state_rows(p, h, halves):
    return pl.ds(pl.multiple_of((p * halves + h) * SUBS, SUBS), SUBS)


def natural_rows(p, tile, halves):
    return pl.ds((p * halves + tile // SUBS) * SUBS + tile % SUBS, SUBS, stride=halves * SUBS)


def token_rows(t):
    return pl.ds(
        lax.shift_right_logical(t, jnp.int32(3)) * (SUBS * SUBS) + lax.bitwise_and(t, jnp.int32(7)),
        SUBS,
        stride=SUBS,
    )


def block_token(b, s):
    return pl.ds(b * (BLOCK * SUBS) + s // SUBS * (SUBS * SUBS) + s % SUBS, SUBS, stride=SUBS)


def saved_rows(b, p, pole_count):
    return pl.ds(pl.multiple_of((b * pole_count + p) * SUBS, SUBS), SUBS)


def block_parts(lo, hi):
    head = jnp.minimum(hi, lax.bitwise_and(lo + (BLOCK - 1), jnp.int32(-BLOCK)))
    shift = jnp.int32(BLOCK.bit_length() - 1)
    first = lax.shift_right_logical(head + (BLOCK - 1), shift)
    last = jnp.maximum(lax.shift_right_logical(hi, shift), first)
    return head, first, last, jnp.maximum(last * BLOCK, head)


def tile_rows(group, j):
    return pl.ds(pl.multiple_of((group * SUBS + j) * SUBS, SUBS), SUBS)


def each_tile(value_ref):
    pole_count, channels = value_ref.shape
    for p in range(0, pole_count, SUBS):
        for tile in range(channels // LANES):
            yield p, tile, (slice(p, p + SUBS), slice(tile * LANES, (tile + 1) * LANES))


def to_states(ref, states, change):
    _, halves = half_span(ref.shape[1])
    for p, tile, at in each_tile(ref):
        states[natural_rows(p, tile, halves), :] = change(at)


def scaled(rate_ref, residue_ref, at):
    return residue_ref[at] * jnp.sqrt(1.0 - jnp.exp(-2.0 * rate_ref[at]))


def chunk_copy(src, src_at, dst, dst_at, sem, start):
    copy = pltpu.make_async_copy(src.at[src_at], dst.at[dst_at], sem)
    if start:
        copy.start()
    else:
        copy.wait()


def token_chunk(c, size=CHUNK):
    return pl.ds(pl.multiple_of(c * size, size), size)


def fill_rows(k_buf, v_buf, u_rows, c, first_tile, width):
    def block(b, _):
        rows = pl.ds(pl.multiple_of(c * LOAD + b * PACKED, PACKED), PACKED)
        for j in range(width):
            lanes = slice((first_tile + j) * LANES, (first_tile + j + 1) * LANES)
            u = k_buf[rows, lanes].astype(F32) * v_buf[rows, lanes].astype(F32)
            for part in range(PACKED // SUBS):
                group = c * (LOAD // SUBS) + b * (PACKED // SUBS) + part
                u_rows[tile_rows(group, j), :] = u[part * SUBS : (part + 1) * SUBS]
        return 0

    lax.fori_loop(0, LOAD // PACKED, block, 0)


def fill_lengths(bounds_ref, lengths_ref):
    for r in range(bounds_ref.shape[0]):
        lengths_ref[r] = jnp.max(bounds_ref[r]).astype(jnp.int32)


def each_request(lengths_ref, base, extent, body):
    def request(r, start):
        length = lengths_ref[r]
        lo = jnp.maximum(start - base, 0)
        hi = jnp.minimum(start + length - base, extent)

        @pl.when(hi > lo)
        def _():
            body(r, start, lo, hi)

        return start + length

    lax.fori_loop(0, lengths_ref.shape[0], request, jnp.int32(0))


def total(terms):
    while len(terms) > 1:
        terms = [x + y for x, y in zip(terms[::2], terms[1::2])] + terms[len(terms) // 2 * 2 :]
    return terms[0]


def pieces_kernel(
    lengths_hbm, owners_hbm, k_hbm, v_hbm, rate_hbm, residue_hbm,
    cross_ref, near_ref, pair_ref, own_ref, mine_ref, bounds_ref, u_rows, decays, gains, saved,
    k_buf, v_buf, rate_ref, residue_ref, lengths_ref, owners_ref, states, sems, small_sems,
):
    n = lax.axis_size("ctx")
    i = lax.axis_index("ctx")
    request_count = lengths_ref.shape[0]
    pole_count, channels = rate_ref.shape
    tok_dev = k_buf.shape[0]
    width, halves = half_span(channels)
    chunks = tok_dev // LOAD
    first = i * tok_dev
    last = first + tok_dev - 1

    def moves(c, start):
        rows = (token_chunk(c, LOAD), slice(None))
        chunk_copy(k_hbm, rows, k_buf, rows, sems.at[0, c], start)
        chunk_copy(v_hbm, rows, v_buf, rows, sems.at[1, c], start)

    small = [
        pltpu.make_async_copy(src, dst, small_sems.at[n])
        for n, (src, dst) in enumerate(
            (
                (lengths_hbm, lengths_ref),
                (owners_hbm, owners_ref),
                (rate_hbm, rate_ref),
                (residue_hbm, residue_ref),
            )
        )
    ]
    for copy in small:
        copy.start()
    for c in range(chunks):
        moves(c, True)

    def clear(b, _):
        states[pl.ds(pl.multiple_of(b * SUBS, SUBS), SUBS), :] = jnp.zeros((SUBS, LANES), F32)
        return 0

    lax.fori_loop(0, request_count * pole_count * halves, clear, 0)
    for copy in small:
        copy.wait()
    for r in range(request_count):
        bounds_ref[r] = jnp.full((SUBS, LANES), lengths_ref[r].astype(F32), F32)
    to_states(rate_ref, decays, lambda at: jnp.exp(-rate_ref[at]))
    to_states(rate_ref, gains, lambda at: scaled(rate_ref, residue_ref, at))

    def chunk(c, _):
        moves(c, False)
        for h in range(halves):
            fill_rows(k_buf, v_buf, u_rows.at[h], c, h * SUBS, width)
        base = c * LOAD

        def request(r, start, lo, hi):
            head, begin, end, tail = block_parts(base + lo, base + hi)

            def half(h, _):
                decay = [decays[state_rows(p, h, halves), :] for p in range(pole_count)]
                row = r * pole_count
                state = tuple(
                    states[state_rows(row + p, h, halves), :] for p in range(pole_count)
                )

                def advance(state, u):
                    return tuple(s * a + u for s, a in zip(state, decay))

                def single(t, state):
                    return advance(state, u_rows[h, token_rows(t), :])

                def save(b, state):
                    for p in range(pole_count):
                        saved[h, saved_rows(b, p, pole_count), :] = state[p]

                def block(b, state):
                    save(b, state)
                    for s in range(BLOCK):
                        state = advance(state, u_rows[h, block_token(b, s), :])
                    return state

                state = lax.fori_loop(base + lo, head, single, state)
                state = lax.fori_loop(begin, end, block, state)

                @pl.when(base + hi > tail)
                def _():
                    save(end, state)

                state = lax.fori_loop(tail, base + hi, single, state)
                for p in range(pole_count):
                    states[state_rows(row + p, h, halves), :] = state[p]
                return 0

            lax.fori_loop(0, halves, half, 0)

        each_request(lengths_ref, first + base, LOAD, request)
        return 0

    lax.fori_loop(0, chunks, chunk, 0)

    def owned(slot):
        request = jnp.int32(0)
        found = jnp.int32(0)
        for r in range(request_count):
            match = (owners_ref[r] == slot).astype(jnp.int32)
            request = request + r * match
            found = found + match
        start, end = request_span(lengths_ref, request, request_count)
        live = (found > 0) & (start <= last) & (end >= first)
        return request, jnp.maximum(end - last, 0), live

    def emit(out_ref, what):
        request, steps, live = what
        back = -steps.astype(F32)
        keep = jnp.where(live, 1.0, 0.0).astype(F32)
        for p, tile, at in each_tile(rate_ref):
            state = states[natural_rows(request * pole_count + p, tile, halves), :]
            out_ref[at] = state * (jnp.exp(rate_ref[at] * back) * keep)

    partner = jnp.where(lax.rem(i, 2) == 1, i - 1, i + 1)
    crossing = request_at(lengths_ref, last, request_count)
    for p, tile, at in each_tile(rate_ref):
        cross_ref[at] = states[natural_rows(crossing * pole_count + p, tile, halves), :]
    emit(near_ref, owned(partner))
    emit(own_ref, owned(i))
    for d in range(1, n // 2):
        emit(pair_ref.at[d - 1], owned(lax.rem(partner + 2 * d, n)))
        emit(mine_ref.at[d - 1], owned(lax.rem(i + 2 * d, n)))


def taps_kernel(bounds_ref, u_rows, decays, gains, skip_ref, y_rows, taps, lengths_ref):
    fill_lengths(bounds_ref, lengths_ref)
    halves = u_rows.shape[0]
    tok_dev = u_rows.shape[1] // SUBS
    pole_count = decays.shape[0] // (halves * SUBS)
    first = lax.axis_index("ctx") * tok_dev

    def half(h, _):
        skip = skip_ref[pl.ds(pl.multiple_of(h * SUBS, SUBS), SUBS), :]
        decay = [decays[state_rows(p, h, halves), :] for p in range(pole_count)]
        power = [gains[state_rows(p, h, halves), :] for p in range(pole_count)]
        for j in range(BLOCK):
            tap = total(list(power))
            taps[j * SUBS : (j + 1) * SUBS, :] = tap + skip if j == 0 else tap
            power = [x * a for x, a in zip(power, decay)]

        def request(r, start, lo, hi):
            head, begin, end, tail = block_parts(lo, hi)

            def alone(lo, hi):
                decay = [decays[state_rows(p, h, halves), :] for p in range(pole_count)]
                gain = [gains[state_rows(p, h, halves), :] for p in range(pole_count)]

                def single(t, state):
                    u = u_rows[h, token_rows(t), :]
                    state = tuple(s * a + u for s, a in zip(state, decay))
                    y_rows[h, token_rows(t), :] = total(
                        [s * g for s, g in zip(state, gain)] + [skip * u]
                    )
                    return state

                zero = jnp.zeros((SUBS, LANES), F32)
                lax.fori_loop(lo, hi, single, (zero,) * pole_count)

            @pl.when(head > lo)
            def _():
                alone(lo, head)

            @pl.when(hi > tail)
            def _():
                alone(tail, hi)

            tap = [taps[j * SUBS : (j + 1) * SUBS, :] for j in range(BLOCK)]

            def block(b, _):
                u = [u_rows[h, block_token(b, s), :] for s in range(BLOCK)]
                for s in range(BLOCK):
                    y_rows[h, block_token(b, s), :] = total(
                        [tap[j] * u[s - j] for j in range(s + 1)]
                    )
                return 0

            lax.fori_loop(begin, end, block, 0)

        each_request(lengths_ref, first, tok_dev, request)
        return 0

    lax.fori_loop(0, halves, half, 0)


def pool_kernel(mine_ref, pair_ref, *pooled_refs):
    for d, ref in enumerate(pooled_refs):
        for _, _, at in each_tile(ref):
            ref[at] = mine_ref[d, at[0], at[1]] + pair_ref[d, at[0], at[1]]


def finish_kernel(late, hops, bounds_ref, y_rows, saved, q_ref, decays, gains, rate_ref, *rest):
    hop_refs = rest[:hops]
    out_hbm, out_buf, w_rows, spread, fading, lengths_ref, out_sems = rest[hops + int(late) :]
    fill_lengths(bounds_ref, lengths_ref)
    tok_dev, channels = q_ref.shape
    halves = y_rows.shape[0]
    pole_count = rate_ref.shape[0]
    width, _ = half_span(channels)
    chunks = tok_dev // CHUNK
    first = lax.axis_index("ctx") * tok_dev
    before = request_before(lengths_ref, tok_dev, 1)
    reached = [
        (before >= 0) & (request_before(lengths_ref, tok_dev, hop) == before)
        for hop in range(1, max(hops, 2) + 1)
    ]
    _, end = request_span(lengths_ref, before, lengths_ref.shape[0])
    split = jnp.where(reached[1], jnp.minimum(end + 1 - first, tok_dev), 0)
    split = lax.div(split + (CHUNK - 1), jnp.int32(CHUNK))
    from_chunk, to_chunk = (0, split) if late else (split, chunks)

    def results(c, start):
        rows = (token_chunk(c), slice(None))
        chunk_copy(out_buf, rows, out_hbm, rows, out_sems.at[c], start)

    def incoming(at):
        state = jnp.zeros((SUBS, LANES), F32)
        for hop, ref in enumerate(hop_refs):
            moved = ref[at] * jnp.exp(rate_ref[at] * -float(hop * tok_dev)) if hop else ref[at]
            state = state + jnp.where(reached[hop], moved, 0.0)
        return state

    @pl.when(from_chunk < to_chunk)
    def _():
        to_states(rate_ref, spread, incoming)
        for p in range(pole_count):
            for h in range(halves):
                at = state_rows(p, h, halves)
                fading[h, state_rows(p, 0, 1), :] = spread[at, :] * gains[at, :] * decays[at, :]

    def gate(c):
        def block(b, _):
            rows = pl.ds(pl.multiple_of(c * CHUNK + b * PACKED, PACKED), PACKED)
            for h in range(halves):
                for j in range(width):
                    lanes = slice((h * SUBS + j) * LANES, (h * SUBS + j + 1) * LANES)
                    w = jnp.concatenate(
                        [
                            w_rows[h, tile_rows(b * (PACKED // SUBS) + part, j), :]
                            for part in range(PACKED // SUBS)
                        ],
                        axis=0,
                    )
                    out_buf[rows, lanes] = (q_ref[rows, lanes].astype(F32) * w).astype(jnp.bfloat16)
            return 0

        lax.fori_loop(0, CHUNK // PACKED, block, 0)

    def chunk(c, _):
        base = c * CHUNK

        def request(r, start, lo, hi):
            head, begin, end, tail = block_parts(lo, hi)

            def half(h, _):
                y = y_rows.at[h, pl.ds(pl.multiple_of(base * SUBS, CHUNK * SUBS), CHUNK * SUBS)]
                w = w_rows.at[h]

                @pl.when(start >= first)
                def _():
                    fading[h] = jnp.zeros(fading.shape[1:], F32)

                def keep(t, _):
                    w[token_rows(t), :] = y[token_rows(t), :]
                    return 0

                lax.fori_loop(lo, head, keep, 0)
                decay = [decays[state_rows(p, h, halves), :] for p in range(pole_count)]

                def opening(b):
                    state = []
                    for p in range(pole_count):
                        at = state_rows(p, h, halves)
                        local = saved[h, saved_rows(base // BLOCK + b, p, pole_count), :]
                        state.append(
                            local * (gains[at, :] * decays[at, :])
                            + fading[h, state_rows(p, 0, 1), :]
                        )
                    return state

                def block(b, _):
                    state = opening(b)
                    for p in range(pole_count):
                        at = state_rows(p, 0, 1)
                        power = decay[p]
                        for _ in range(BLOCK.bit_length() - 1):
                            power = power * power
                        fading[h, at, :] = fading[h, at, :] * power
                    for s in range(BLOCK):
                        rows = block_token(b, s)
                        w[rows, :] = y[rows, :] + total(list(state))
                        if s < BLOCK - 1:
                            state = [x * a for x, a in zip(state, decay)]
                    return 0

                lax.fori_loop(begin, end, block, 0)

                @pl.when(hi > tail)
                def _():
                    def single(t, state):
                        w[token_rows(t), :] = y[token_rows(t), :] + total(list(state))
                        return tuple(x * a for x, a in zip(state, decay))

                    lax.fori_loop(tail, hi, single, tuple(opening(end)))

                return 0

            lax.fori_loop(0, halves, half, 0)

        each_request(lengths_ref, first + base, CHUNK, request)
        gate(c)
        results(c, True)
        return 0

    def drain(c, _):
        results(c, False)
        return 0

    lax.fori_loop(from_chunk, to_chunk, chunk, 0)
    lax.fori_loop(from_chunk, to_chunk, drain, 0)


SMEM = pl.BlockSpec(memory_space=pltpu.SMEM)
VMEM = pl.BlockSpec(memory_space=pltpu.VMEM)
HBM = pl.BlockSpec(memory_space=pltpu.HBM)
DMA = pltpu.SemaphoreType.DMA


def in_hbm(x):
    return pltpu.with_memory_space_constraint(x, pltpu.HBM)


def call(kernel, name, out_shape, in_specs, out_specs, scratch=(), cost=(0, 0), aliases=None):
    return pl.pallas_call(
        kernel,
        out_shape=out_shape,
        in_specs=in_specs,
        out_specs=out_specs,
        scratch_shapes=list(scratch),
        compiler_params=pltpu.CompilerParams(vmem_limit_bytes=VMEM_BYTES),
        cost_estimate=pl.CostEstimate(flops=cost[0], bytes_accessed=cost[1], transcendentals=0),
        input_output_aliases=aliases or {},
        name=name,
    )


def rotate(block, distance):
    n = lax.axis_size("ctx")
    return lax.ppermute(block, "ctx", [(i, (i + distance) % n) for i in range(n)])


def trade(block):
    n = lax.axis_size("ctx")
    return lax.ppermute(block, "ctx", [(i, i ^ 1) for i in range(n)])


def shards(q_feat, k_feat, v_feat, pole_rate, residue, skip_gain, lengths, owners):
    tok_dev, channels = q_feat.shape
    pole_count = pole_rate.shape[0]
    request_count = lengths.shape[0]
    n = lax.axis_size("ctx")
    width, halves = half_span(channels)
    chunks = tok_dev // CHUNK
    longest = n * tok_dev // 2
    hops = -(-(longest - 1) // tok_dev)
    element = tok_dev * channels * pole_count
    token_bytes = tok_dev * channels
    one = jax.ShapeDtypeStruct((pole_count, channels), F32)
    all_rows = jax.ShapeDtypeStruct((halves, tok_dev * SUBS, LANES), F32)
    state_shape = jax.ShapeDtypeStruct((pole_count * halves * SUBS, LANES), F32)
    saved_shape = jax.ShapeDtypeStruct(
        (halves, tok_dev // BLOCK * pole_count * SUBS, LANES), F32
    )
    tokens = pltpu.VMEM((tok_dev, channels), jnp.bfloat16)

    def blocks(count):
        return jax.ShapeDtypeStruct((count, pole_count, channels), F32)

    cross, near_out, pair_out, own, mine, bounds, u_rows, decays, gains, saved = call(
        pieces_kernel,
        "pieces",
        [one, one, blocks(n // 2 - 1), one, blocks(n // 2 - 1)]
        + [jax.ShapeDtypeStruct((request_count, SUBS, LANES), F32), all_rows, state_shape, state_shape, saved_shape],
        [HBM] * 6,
        [VMEM] * 10,
        [
            tokens,
            tokens,
            pltpu.VMEM((pole_count, channels), F32),
            pltpu.VMEM((pole_count, channels), F32),
            pltpu.SMEM((request_count,), jnp.int32),
            pltpu.SMEM((request_count,), jnp.int32),
            pltpu.VMEM((request_count * pole_count * halves * SUBS, LANES), F32),
            DMA((2, tok_dev // LOAD)),
            DMA((4,)),
        ],
        (2 * element, 8 * token_bytes),
    )(*map(in_hbm, (lengths, owners, k_feat, v_feat, pole_rate, residue)))

    hop_in = [rotate(cross, 1)]
    pair_in = trade(pair_out)
    hop_in += [rotate(cross, hop) for hop in range(2, hops + 1)]

    skip_rows = skip_gain.reshape(-1, LANES)
    if skip_rows.shape[0] < SUBS:
        skip_rows = jnp.pad(skip_rows, ((0, SUBS - skip_rows.shape[0]), (0, 0)))
    y_rows = call(
        taps_kernel,
        "taps",
        all_rows,
        [VMEM] * 5,
        VMEM,
        [pltpu.VMEM((BLOCK * SUBS, LANES), F32), pltpu.SMEM((request_count,), jnp.int32)],
        (BLOCK * token_bytes, 8 * token_bytes),
    )(bounds, u_rows, decays, gains, skip_rows)

    near_out, y_rows = lax.optimization_barrier((near_out, y_rows))
    near_in = trade(near_out)
    pair_in, y_rows = lax.optimization_barrier((pair_in, y_rows))
    far_out = call(
        pool_kernel, "pool", [one] * (n // 2 - 1), [VMEM] * 2, [VMEM] * (n // 2 - 1)
    )(mine, pair_in)
    far_in = [rotate(block, 2 * d) for d, block in enumerate(far_out, 1)]

    mixed_shape = jax.ShapeDtypeStruct((tok_dev, channels), jnp.bfloat16)

    def finish(late, used, more):
        operands = [bounds, y_rows, saved, q_feat, decays, gains, pole_rate, *used]
        return call(
            functools.partial(finish_kernel, late, len(used)),
            "late" if late else "finish",
            mixed_shape,
            [VMEM] * (7 + len(used)) + [HBM] * len(more),
            HBM,
            [
                tokens,
                pltpu.VMEM((halves, CHUNK * SUBS, LANES), F32),
                pltpu.VMEM(state_shape.shape, F32),
                pltpu.VMEM((halves, pole_count * SUBS, LANES), F32),
                pltpu.SMEM((request_count,), jnp.int32),
                DMA((chunks,)),
            ],
            (2 * element, 8 * token_bytes),
            {len(operands): 0} if late else None,
        )(*operands, *more)

    mixed_out = finish(True, hop_in, [finish(False, hop_in[:1], [])])
    return mixed_out, sum(far_in, own + near_in)[None]


def solution(mesh):
    placed = (
        P(("groups", "ctx"), "chan"),
        P(("groups", "ctx"), "chan"),
        P(("groups", "ctx"), "chan"),
        P(None, "chan"),
        P(None, "chan"),
        P("chan"),
        P("groups"),
        P("groups"),
    )
    return jax.shard_map(
        shards,
        mesh=mesh,
        in_specs=placed,
        out_specs=(P(("groups", "ctx"), "chan"), P(("groups", "ctx"), None, "chan")),
        check_vma=False,
    )
```
